32 devices in a mesh: groups: 2 (over y), rep: 4 (over x, core), tp: 4 (over z).
Axes of the slice: x: 2, y: 2, z: 4, core: 2. Of those that a mesh axis runs over, the one named last changes fastest.
Arguments:
- base: bfloat16 [16384, 40960], P('tp', 'rep'), may hold values from -0.046875 to 0.046875
- decoded_row_activations: bfloat16 [512, 16384], P('groups', 'tp'), parts along dimension 0, may hold values from -6 to 6
- input_factor: float32 [32768, 32], P(('groups', 'tp'), 'rep'), parts along dimension 0, may hold values from -0.046875 to 0.046875
- output_factor: float32 [32, 81920], P('rep', ('groups', 'tp')), parts along dimension 1, may hold values from -0.3125 to 0.3125
- input_first_moment: float32 [32768, 32], P(('groups', 'tp'), 'rep'), parts along dimension 0, may hold values from -4 to 4
- input_second_moment: float32 [32768, 32], P(('groups', 'tp'), 'rep'), parts along dimension 0, may hold values from 0.02 to 0.5
- output_first_moment: float32 [32, 81920], P('rep', ('groups', 'tp')), parts along dimension 1, may hold values from -4 to 4
- output_second_moment: float32 [32, 81920], P('rep', ('groups', 'tp')), parts along dimension 1, may hold values from 0.02 to 0.5
- replica_input_gradient: float32 [4, 32768, 32], P('rep', ('groups', 'tp')), parts along dimension 1, may hold values from -4 to 4
- replica_output_gradient: float32 [4, 32, 81920], P('rep', None, ('groups', 'tp')), parts along dimension 2, may hold values from -4 to 4
Outputs:
- decoded: float32 [512, 40960], P(('groups', 'tp'), 'rep'), parts along dimension 0
- lora_in_new: float32 [32768, 32], P(('groups', 'tp'), 'rep'), parts along dimension 0
- lora_out_new: float32 [32, 81920], P('rep', ('groups', 'tp')), parts along dimension 1
- input_first_moment_next: float32 [32768, 32], P(('groups', 'tp'), 'rep'), parts along dimension 0
- input_second_moment_next: float32 [32768, 32], P(('groups', 'tp'), 'rep'), parts along dimension 0
- output_first_moment_next: float32 [32, 81920], P('rep', ('groups', 'tp')), parts along dimension 1
- output_second_moment_next: float32 [32, 81920], P('rep', ('groups', 'tp')), parts along dimension 1
The draws below stay inside these ranges and needn't reach their ends.
There are 2 independent parts, one for each index of `groups`. The reference program is written for one: setup_inputs(seed, part) draws one part's arguments, and reference() takes and returns one part's arrays. A program takes and returns all parts, laid end to end along the dimension named above; an argument that names none is the same for every part. Nothing has to cross between parts.
All inputs are finite; a program needn't handle non-finite values.
Results may differ from the reference program's by a relative error of at most 0.0031.
Values may be sent and summed in bfloat16 or wider, within the bound.
No kernel may reach another device: no remote copies, remote signals or barrier semaphores. Data moves between devices by JAX's collectives and lax.ppermute only.
A program may use at most 256 MiB of HBM per device.

```python
import math
import jax
import jax.numpy as jnp
from jax import lax

MODEL_WIDTH = 16384
HIDDEN_WINDOW = 40960
FACTOR_RANK = 32
ROWS = 256
ADAM_STEP = 200
REPLICAS = 4
N_REP = 4
N_TP = 4


def level_of(rng, dims, cuts, least, top_value):
    loudness = 1.0
    for axis_at, blocks in cuts:
        steps = jax.random.uniform(jax.random.fold_in(jax.random.fold_in(rng, 6), axis_at), (blocks,), jnp.float32, least / len(cuts), top_value / len(cuts))
        loudness = loudness * jnp.repeat(jnp.exp(steps), dims[axis_at] // blocks).reshape((-1,) + (1,) * (len(dims) - 1 - axis_at))
    return loudness


def noise(own_key, dims, spread, most, cuts=(), kind=jnp.bfloat16):
    array = spread * jax.random.normal(own_key, dims, jnp.float32)
    if cuts:
        array = array * level_of(own_key, dims, cuts, -0.22, 0.18)
    return jnp.clip(array, -most, most).astype(kind)


def setup_inputs(seed: int = 0, part: int = 0) -> dict:
    keys = jax.random.split(jax.random.key(seed), 11)
    part_keys = jax.random.split(jax.random.fold_in(keys[10], part), 11)
    return {
        "base": noise(keys[0], (MODEL_WIDTH, HIDDEN_WINDOW), MODEL_WIDTH ** -0.5, 0.046875, ((0, 4), (1, 4))),
        "decoded_row_activations": noise(part_keys[1], (ROWS, MODEL_WIDTH), 1.0, 6.0, ((1, 4),)),
        "input_factor": noise(part_keys[2], (MODEL_WIDTH, FACTOR_RANK), MODEL_WIDTH ** -0.5, 0.046875, ((0, 4), (1, 4)), jnp.float32),
        "output_factor": noise(part_keys[3], (FACTOR_RANK, HIDDEN_WINDOW), 0.02, 0.3125, ((0, 4), (1, 4)), jnp.float32),
        "input_first_moment": noise(part_keys[4], (MODEL_WIDTH, FACTOR_RANK), 0.3, 4.0, ((0, 4), (1, 4)), jnp.float32),
        "input_second_moment": jnp.clip(jnp.exp(math.log(0.5) - 3.218876 * jax.random.uniform(part_keys[5], (MODEL_WIDTH, FACTOR_RANK), jnp.float32) ** level_of(part_keys[5], (MODEL_WIDTH, FACTOR_RANK), ((0, 4), (1, 4)), -0.2, 0.2)), 0.02, 0.5),
        "output_first_moment": noise(part_keys[6], (FACTOR_RANK, HIDDEN_WINDOW), 0.3, 4.0, ((0, 4), (1, 4)), jnp.float32),
        "output_second_moment": jnp.clip(jnp.exp(math.log(0.5) - 3.218876 * jax.random.uniform(part_keys[7], (FACTOR_RANK, HIDDEN_WINDOW), jnp.float32) ** level_of(part_keys[7], (FACTOR_RANK, HIDDEN_WINDOW), ((0, 4), (1, 4)), -0.2, 0.2)), 0.02, 0.5),
        "replica_input_gradient": noise(part_keys[8], (REPLICAS, MODEL_WIDTH, FACTOR_RANK), 0.3, 4.0, ((0, 4), (1, 4)), jnp.float32),
        "replica_output_gradient": noise(part_keys[9], (REPLICAS, FACTOR_RANK, HIDDEN_WINDOW), 0.3, 4.0, ((0, 4), (2, 4)), jnp.float32),
    }


beta_one = 0.9
beta_two = 0.999
learn_rate = 0.003
adam_eps = 1e-08
factor_scale = 2.0

def apply_adam_rule(weights, moment, second, grads):
    moment_new = beta_one * moment + (1.0 - beta_one) * grads
    second_new = beta_two * second + (1.0 - beta_two) * grads * grads
    first_fix = 1.0 - beta_one ** ADAM_STEP
    second_fix = 1.0 - beta_two ** ADAM_STEP
    step_size = moment_new / first_fix / (jnp.sqrt(second_new / second_fix) + adam_eps)
    return (weights - learn_rate * step_size, moment_new, second_new)

def reference(base, decoded_row_activations, input_factor, output_factor, input_first_moment, input_second_moment, output_first_moment, output_second_moment, replica_input_gradient, replica_output_gradient):
    input_gradient_sum = lax.optimization_barrier(jnp.sum(replica_input_gradient, axis=0))
    output_gradient_sum = lax.optimization_barrier(jnp.sum(replica_output_gradient, axis=0))
    refreshed_input_factor, input_first_moment_next, input_second_moment_next = apply_adam_rule(input_factor, input_first_moment, input_second_moment, input_gradient_sum)
    refreshed_output_factor, output_first_moment_next, output_second_moment_next = apply_adam_rule(output_factor, output_first_moment, output_second_moment, output_gradient_sum)
    half_in = refreshed_input_factor.astype(jnp.bfloat16)
    half_out = refreshed_output_factor.astype(jnp.bfloat16)
    blocks = N_REP * N_TP
    width = HIDDEN_WINDOW // blocks

    def one_block(index):
        start = (index * width).astype(jnp.int32)
        frozen_columns = lax.dynamic_slice_in_dim(base, start, width, 1)
        out_cols = lax.dynamic_slice_in_dim(half_out, start, width, 1)
        weight_change = jnp.dot(half_in, out_cols, preferred_element_type=jnp.float32)
        merged_weight = (frozen_columns.astype(jnp.float32) + factor_scale * weight_change).astype(jnp.bfloat16)
        return jnp.dot(decoded_row_activations, merged_weight, preferred_element_type=jnp.float32)
    pieces = lax.map(one_block, jnp.arange(blocks, dtype=jnp.int32))
    decoded = jnp.transpose(pieces, (1, 0, 2)).reshape(ROWS, HIDDEN_WINDOW)
    return (decoded, refreshed_input_factor, refreshed_output_factor, input_first_moment_next, input_second_moment_next, output_first_moment_next, output_second_moment_next)
```

```python
import jax
import jax.numpy as jnp
from jax import lax
from jax.sharding import PartitionSpec as P

ADAM_STEP = 200


beta_one = 0.9
beta_two = 0.999
learn_rate = 0.003
adam_eps = 1e-08
factor_scale = 2.0

CHUNKS = (1, 3, 4, 4, 4, 3, 1)


def apply_adam_rule(weights, moment, second, grads):
    moment_new = beta_one * moment + (1.0 - beta_one) * grads
    second_new = beta_two * second + (1.0 - beta_two) * grads * grads
    first_fix = 1.0 - beta_one**ADAM_STEP
    second_fix = 1.0 - beta_two**ADAM_STEP
    step_size = moment_new / first_fix / (jnp.sqrt(second_new / second_fix) + adam_eps)
    return (weights - learn_rate * step_size, moment_new, second_new)


def scatter_sum_rep(part):
    reps = lax.axis_size("rep")
    me = lax.axis_index("rep")
    share = part.shape[0] // reps
    blocks = part.reshape(reps, share, part.shape[1])
    bit = 1
    while bit < reps:
        pairs = blocks.reshape(blocks.shape[0] // 2, 2, share, part.shape[1])
        mine_bit = (me // bit) % 2
        keep = lax.dynamic_index_in_dim(pairs, mine_bit, 1, keepdims=False)
        send = lax.dynamic_index_in_dim(pairs, 1 - mine_bit, 1, keepdims=False)
        got = lax.ppermute(send.astype(jnp.bfloat16), "rep", [(i, i ^ bit) for i in range(reps)])
        blocks = keep + got.astype(jnp.float32)
        bit *= 2
    return blocks[0]


def split_high_low(values):
    high = values.astype(jnp.bfloat16)
    low = (values - high.astype(jnp.float32)).astype(jnp.bfloat16)
    return high, low


def after(value, *earlier):
    return lax.optimization_barrier((value,) + earlier)[0]


def line_step(k, partial, arrived, me, size, share):
    rows = (size - k) * share
    rightward = me == k - 1
    outgoing = lax.dynamic_slice_in_dim(partial, jnp.where(rightward, k * share, 0), rows, 0)
    if arrived is not None:
        passed = lax.dynamic_slice_in_dim(arrived, jnp.where(rightward, share, 0), rows, 0)
        outgoing = outgoing + passed.astype(jnp.float32)
    return lax.ppermute(outgoing.astype(jnp.bfloat16), "tp", [(k - 1, k), (size - k, size - k - 1)])


def line_total(partial, arrivals, me, size, share):
    total = lax.dynamic_slice_in_dim(partial, me * share, share, 0)
    for k, arrived in enumerate(arrivals, 1):
        offset = jnp.where(me == k, 0, (size - 1 - k) * share)
        total = total + lax.dynamic_slice_in_dim(arrived, offset, share, 0).astype(jnp.float32)
    return total


def chunk_bounds(width, weights):
    unit = width // sum(weights)
    bounds = [0]
    for weight in weights:
        bounds.append(bounds[-1] + weight * unit)
    bounds[-1] = width
    return bounds


def local(
    base,
    decoded_row_activations,
    input_factor,
    output_factor,
    input_first_moment,
    input_second_moment,
    output_first_moment,
    output_second_moment,
    replica_input_gradient,
    replica_output_gradient,
):
    x = decoded_row_activations
    width = base.shape[1]
    features = base.shape[0]
    reps, tps = lax.axis_size("rep"), lax.axis_size("tp")
    share = x.shape[0] // tps
    me = lax.axis_index("tp")
    in_line = tps in (2, 4)

    bounds = chunk_bounds(width, CHUNKS)
    partials, firsts = [], []
    previous = None
    for start, stop in zip(bounds[:-1], bounds[1:]):
        rows = x if previous is None else after(x, previous)
        partial = jnp.dot(rows, base[:, start:stop], preferred_element_type=jnp.float32)
        partials.append(partial)
        previous = partial
        if in_line:
            firsts.append(line_step(1, partial, None, me, tps, share))

    part = jnp.concatenate([replica_input_gradient[0].T, replica_output_gradient[0]], axis=1)
    part = after(part, partials[0])
    grads = scatter_sum_rep(part)
    grads_in, grads_out = grads[:, :features], grads[:, features:]
    new_in, first_in, second_in = apply_adam_rule(input_factor.T, input_first_moment.T, input_second_moment.T, grads_in)
    new_out, first_out, second_out = apply_adam_rule(output_factor, output_first_moment, output_second_moment, grads_out)
    half_in = new_in.astype(jnp.bfloat16)
    half_out = new_out.astype(jnp.bfloat16)

    inner = lax.dot_general(x, half_in, (((1,), (1,)), ((), ())), preferred_element_type=jnp.float32)
    inner = lax.psum_scatter(inner, "tp", scatter_dimension=0, tiled=True)
    inner = lax.all_gather(inner, "rep", axis=1, tiled=True)
    if reps == tps:
        turned = lax.ppermute(
            half_out, ("rep", "tp"), [(a * tps + b, b * tps + a) for a in range(reps) for b in range(tps)]
        )
        full_out = lax.all_gather(turned, "tp", axis=0, tiled=True)
    else:
        gathered = lax.all_gather(half_out, ("rep", "tp"), axis=1, tiled=True)
        stacked = gathered.reshape(half_out.shape[0], reps, -1)
        full_out = jnp.transpose(stacked, (1, 0, 2)).reshape(half_out.shape[0] * reps, -1)
        full_out = lax.dynamic_slice_in_dim(full_out, lax.axis_index("rep") * width, width, 1)

    high, low = split_high_low(factor_scale * inner)
    spread = jnp.concatenate([high, low], axis=1)
    doubled = jnp.concatenate([full_out, full_out], axis=0)
    decoded = jnp.zeros((share, width), jnp.float32)
    for index, (start, stop) in enumerate(zip(bounds[:-1], bounds[1:])):
        partial = partials[index]
        if in_line:
            arrivals = [firsts[index]]
            for k in range(2, tps):
                arrivals.append(line_step(k, partial, arrivals[-1], me, tps, share))
            total = line_total(partial, arrivals, me, tps, share)
        else:
            total = lax.psum_scatter(partial, "tp", scatter_dimension=0, tiled=True)
        change = jnp.dot(spread, doubled[:, start:stop], preferred_element_type=jnp.float32)
        decoded = lax.dynamic_update_slice(decoded, total + change, (0, start))
    return (decoded, new_in.T, new_out, first_in.T, second_in.T, first_out, second_out)


def solution(mesh):
    return jax.shard_map(
        local,
        mesh=mesh,
        in_specs=(
            P("tp", "rep"),
            P("groups", "tp"),
            P(("groups", "tp"), "rep"),
            P("rep", ("groups", "tp")),
            P(("groups", "tp"), "rep"),
            P(("groups", "tp"), "rep"),
            P("rep", ("groups", "tp")),
            P("rep", ("groups", "tp")),
            P("rep", ("groups", "tp"), None),
            P("rep", None, ("groups", "tp")),
        ),
        out_specs=(
            P(("groups", "tp"), "rep"),
            P(("groups", "tp"), "rep"),
            P("rep", ("groups", "tp")),
            P(("groups", "tp"), "rep"),
            P(("groups", "tp"), "rep"),
            P("rep", ("groups", "tp")),
            P("rep", ("groups", "tp")),
        ),
        check_vma=False,
    )
```

```python
import jax
import jax.numpy as jnp
from jax import lax
from jax.experimental import pallas as pl
from jax.experimental.pallas import tpu as pltpu
from jax.sharding import PartitionSpec as P

ADAM_STEP = 200


beta_one = 0.9
beta_two = 0.999
learn_rate = 0.003
adam_eps = 1e-08
factor_scale = 2.0

CHUNKS = (1, 3, 6, 6, 3, 1)
VMEM_BYTES = 40 * 1024 * 1024


def apply_adam_rule(weights, moment, second, grads):
    moment_new = beta_one * moment + (1.0 - beta_one) * grads
    second_new = beta_two * second + (1.0 - beta_two) * grads * grads
    first_fix = 1.0 - beta_one**ADAM_STEP
    second_fix = 1.0 - beta_two**ADAM_STEP
    step_size = moment_new / first_fix / (jnp.sqrt(second_new / second_fix) + adam_eps)
    return (weights - learn_rate * step_size, moment_new, second_new)


def scatter_sum_rep(part):
    reps = lax.axis_size("rep")
    me = lax.axis_index("rep")
    share = part.shape[0] // reps
    blocks = part.reshape(reps, share, part.shape[1])
    bit = 1
    while bit < reps:
        pairs = blocks.reshape(blocks.shape[0] // 2, 2, share, part.shape[1])
        mine_bit = (me // bit) % 2
        keep = lax.dynamic_index_in_dim(pairs, mine_bit, 1, keepdims=False)
        send = lax.dynamic_index_in_dim(pairs, 1 - mine_bit, 1, keepdims=False)
        got = lax.ppermute(send.astype(jnp.bfloat16), "rep", [(i, i ^ bit) for i in range(reps)])
        blocks = keep + got.astype(jnp.float32)
        bit *= 2
    return blocks[0]


def split_high_low(values):
    high = values.astype(jnp.bfloat16)
    low = (values - high.astype(jnp.float32)).astype(jnp.bfloat16)
    return high, low


def local_any(
    base,
    decoded_row_activations,
    input_factor,
    output_factor,
    input_first_moment,
    input_second_moment,
    output_first_moment,
    output_second_moment,
    replica_input_gradient,
    replica_output_gradient,
):
    x = decoded_row_activations
    width = base.shape[1]
    features = base.shape[0]
    reps = lax.axis_size("rep")
    part = jnp.concatenate([replica_input_gradient[0].T, replica_output_gradient[0]], axis=1)
    grads = scatter_sum_rep(part)
    grads_in, grads_out = grads[:, :features], grads[:, features:]
    new_in, first_in, second_in = apply_adam_rule(input_factor.T, input_first_moment.T, input_second_moment.T, grads_in)
    new_out, first_out, second_out = apply_adam_rule(output_factor, output_first_moment, output_second_moment, grads_out)
    half_in = new_in.astype(jnp.bfloat16)
    half_out = new_out.astype(jnp.bfloat16)
    inner = lax.dot_general(x, half_in, (((1,), (1,)), ((), ())), preferred_element_type=jnp.float32)
    inner = lax.psum_scatter(inner, "tp", scatter_dimension=0, tiled=True)
    inner = lax.all_gather(inner, "rep", axis=1, tiled=True)
    gathered = lax.all_gather(half_out, ("rep", "tp"), axis=1, tiled=True)
    stacked = gathered.reshape(half_out.shape[0], reps, -1)
    full_out = jnp.transpose(stacked, (1, 0, 2)).reshape(half_out.shape[0] * reps, -1)
    full_out = lax.dynamic_slice_in_dim(full_out, lax.axis_index("rep") * width, width, 1)
    high, low = split_high_low(factor_scale * inner)
    spread = jnp.concatenate([high, low], axis=1)
    doubled = jnp.concatenate([full_out, full_out], axis=0)
    partial = jnp.dot(x, base, preferred_element_type=jnp.float32)
    summed = lax.psum_scatter(partial, "tp", scatter_dimension=0, tiled=True)
    decoded = summed + jnp.dot(spread, doubled, preferred_element_type=jnp.float32)
    return (decoded, new_in.T, new_out, first_in.T, second_in.T, first_out, second_out)


LINE = (((0, 1), (3, 2)), ((1, 2), (2, 1)), ((2, 3), (1, 0)))
(SEND_ROW, SECOND_AT, THIRD_AT, THIRD_FROM, OWN, FIRST_OWN, SECOND_OWN, ORDER, CORE_BIT, CHIP_BIT) = (
    0, 1, 2, 3, 4, 5, 6, 7, 11, 12)


def place_numbers(share):
    me, rep = lax.axis_index("tp"), lax.axis_index("rep")
    low = me < 2
    order = [me, me ^ 1, jnp.where(low, 2, 1), jnp.where(low, 3, 0)]
    numbers = [
        jnp.where(me == 0, share, 0),
        jnp.where(me == 1, 1, 0),
        jnp.where(me == 2, 3, 0),
        jnp.where(me == 2, 1, 0),
        me,
        jnp.where(me == 1, 0, 2),
        jnp.where(me == 2, 0, 1),
    ]
    numbers += [rank ^ rep for rank in order] + [rep & 1, rep >> 1]
    return jnp.stack([jnp.asarray(n, jnp.int32) for n in numbers])


def call(body, place, operands, specs, earlier, out_shapes, out_specs, grid=(1,), flops=0, moved=0, aliases=None):
    count = len(operands)

    def kernel(place_ref, *refs):
        body(place_ref, *refs[:count], *refs[count + len(earlier):])

    return pl.pallas_call(
        kernel,
        grid_spec=pltpu.PrefetchScalarGridSpec(
            num_scalar_prefetch=1,
            grid=grid,
            in_specs=list(specs) + [pl.BlockSpec(memory_space=pl.ANY)] * len(earlier),
            out_specs=out_specs,
        ),
        out_shape=out_shapes,
        input_output_aliases={} if aliases is None else aliases,
        compiler_params=pltpu.CompilerParams(vmem_limit_bytes=VMEM_BYTES),
        cost_estimate=pl.CostEstimate(flops=flops, bytes_accessed=moved, transcendentals=0),
    )(place, *operands, *earlier)


def whole(shape):
    return pl.BlockSpec(shape, lambda *_: (0,) * len(shape))


def block_width(start, width, most):
    block = most
    while start % block or width % block:
        block //= 2
    return block


def matmul_chunk(place, x, base, start, width, share, earlier, most):
    rows, depth = x.shape
    block = block_width(start, width, most)
    sent = rows - share

    def body(place_ref, x_ref, base_ref, partial_ref, send_ref):
        partial_ref[...] = jnp.dot(x_ref[...], base_ref[...], preferred_element_type=jnp.float32)
        row = pl.multiple_of(place_ref[SEND_ROW], share)
        send_ref[...] = partial_ref[pl.ds(row, sent), :].astype(jnp.bfloat16)

    return call(
        body,
        place,
        [x, base],
        [whole(x.shape), pl.BlockSpec((depth, block), lambda j, p: (0, start // block + j))],
        earlier,
        [jax.ShapeDtypeStruct((rows, width), jnp.float32), jax.ShapeDtypeStruct((sent, width), jnp.bfloat16)],
        [pl.BlockSpec((rows, block), lambda j, p: (0, j)), pl.BlockSpec((sent, block), lambda j, p: (0, j))],
        grid=(width // block,),
        flops=2 * rows * depth * width,
        moved=2 * depth * width,
    )


def add_second(place, partial, arrived, share, earlier):
    width = partial.shape[1]
    block = block_width(0, width, 1024) if width % 128 == 0 else width

    def body(place_ref, partial_ref, upper_ref, lower_ref, out_ref):
        out_ref[:share, :] = (partial_ref[:share, :] + upper_ref[...].astype(jnp.float32)).astype(out_ref.dtype)
        out_ref[share:, :] = (partial_ref[share:, :] + lower_ref[...].astype(jnp.float32)).astype(out_ref.dtype)

    return call(
        body,
        place,
        [partial, arrived, arrived],
        [
            pl.BlockSpec((2 * share, block), lambda j, p: (p[SECOND_AT], j)),
            pl.BlockSpec((share, block), lambda j, p: (p[SECOND_AT], j)),
            pl.BlockSpec((share, block), lambda j, p: (p[SECOND_AT] + 1, j)),
        ],
        earlier,
        jax.ShapeDtypeStruct((2 * share, width), arrived.dtype),
        pl.BlockSpec((2 * share, block), lambda j, p: (0, j)),
        grid=(width // block,),
        moved=16 * share * width,
    )


def add_third(place, partial, arrived, share, earlier):
    width = partial.shape[1]
    block = block_width(0, width, 1024) if width % 128 == 0 else width

    def body(place_ref, partial_ref, arrived_ref, out_ref):
        out_ref[...] = (partial_ref[...] + arrived_ref[...].astype(jnp.float32)).astype(out_ref.dtype)

    return call(
        body,
        place,
        [partial, arrived],
        [
            pl.BlockSpec((share, block), lambda j, p: (p[THIRD_AT], j)),
            pl.BlockSpec((share, block), lambda j, p: (p[THIRD_FROM], j)),
        ],
        earlier,
        jax.ShapeDtypeStruct((share, width), arrived.dtype),
        pl.BlockSpec((share, block), lambda j, p: (0, j)),
        grid=(width // block,),
        moved=8 * share * width,
    )


def own_block_specs(share, block):
    return [
        pl.BlockSpec((share, block), lambda j, p: (p[OWN], j)),
        pl.BlockSpec((share, block), lambda j, p: (p[FIRST_OWN], j)),
        pl.BlockSpec((share, block), lambda j, p: (p[SECOND_OWN], j)),
        pl.BlockSpec((share, block), lambda j, p: (0, j)),
    ]


def own_total(refs):
    total = refs[0][...]
    for ref in refs[1:]:
        total = total + ref[...].astype(jnp.float32)
    return total


def finish_chunk(place, terms, spread, factors, decoded, start, width, share, full_width, earlier):
    block = block_width(start, width, 1024)
    first = start // block
    operands = [*terms, spread, *factors]

    def body(place_ref, own_ref, one_ref, two_ref, three_ref, spread_ref, pair_ref, near_ref, far_ref, *rest):
        other = near_ref[...] + far_ref[...]
        ranks = jnp.concatenate([pair_ref[...], other, pair_ref[...], other], axis=0)
        change = jnp.dot(spread_ref[...], ranks, preferred_element_type=jnp.float32)
        rest[-1][...] = own_total((own_ref, one_ref, two_ref, three_ref)) + change

    half = factors[0].shape[0]
    specs = own_block_specs(share, block) + [whole(spread.shape)]
    specs += [pl.BlockSpec((half, block), lambda j, p: (0, first + j))] * 3
    aliases = None
    if decoded is not None:
        aliases = {1 + len(operands): 0}
        operands.append(decoded)
        specs.append(pl.BlockSpec(memory_space=pl.ANY))
    return call(
        body,
        place,
        operands,
        specs,
        earlier,
        jax.ShapeDtypeStruct((share, full_width), jnp.float32),
        pl.BlockSpec((share, block), lambda j, p: (0, first + j)),
        grid=(width // block,),
        moved=14 * share * width,
        aliases=aliases,
    )


def gradients_out(place, part_in, part_out, earlier):
    features, columns = part_in.shape[3], part_out.shape[3]
    rows = 2 * part_in.shape[2]

    def body(place_ref, in_ref, out_ref, send_ref):
        send_ref[:, :features] = in_ref[...].reshape(rows, features).astype(jnp.bfloat16)
        send_ref[:, features:] = out_ref[...].reshape(rows, columns).astype(jnp.bfloat16)

    shape = (rows, features + columns)
    return call(
        body,
        place,
        [part_in, part_out],
        [
            pl.BlockSpec((2, 1, rows // 2, n), lambda j, p: (0, 1 - p[CORE_BIT], 0, 0))
            for n in (features, columns)
        ],
        earlier,
        jax.ShapeDtypeStruct(shape, jnp.bfloat16),
        whole(shape),
        moved=6 * shape[0] * shape[1],
    )


def gradients_on(place, part_in, part_out, arrived, earlier):
    features, columns = part_in.shape[3], part_out.shape[3]
    ranks = part_in.shape[2]

    def body(place_ref, in_ref, out_ref, arrived_ref, send_ref, keep_ref):
        upper = place_ref[CHIP_BIT] == 0
        for ref, at, n in ((in_ref, 0, features), (out_ref, features, columns)):
            total = ref[...].reshape(2 * ranks, n) + arrived_ref[:, at:at + n].astype(jnp.float32)
            keep_ref[:, at:at + n] = jnp.where(upper, total[:ranks], total[ranks:])
            send_ref[:, at:at + n] = jnp.where(upper, total[ranks:], total[:ranks]).astype(jnp.bfloat16)

    shape = (ranks, features + columns)
    return call(
        body,
        place,
        [part_in, part_out, arrived],
        [pl.BlockSpec((2, 1, ranks, n), lambda j, p: (0, p[CORE_BIT], 0, 0)) for n in (features, columns)]
        + [whole(arrived.shape)],
        earlier,
        [jax.ShapeDtypeStruct(shape, jnp.bfloat16), jax.ShapeDtypeStruct(shape, jnp.float32)],
        [whole(shape)] * 2,
        moved=20 * shape[0] * shape[1],
    )


def update_factors(place, keep, arrived, in_state, out_state, earlier):
    features, columns = in_state[0].shape[1], out_state[0].shape[1]
    ranks = keep.shape[0]

    def body(place_ref, keep_ref, arrived_ref, *refs):
        for side, at, n in ((0, 0, features), (1, features, columns)):
            weights, first, second = refs[3 * side:3 * side + 3]
            outs = refs[6 + 4 * side:10 + 4 * side]
            grads = keep_ref[:, at:at + n] + arrived_ref[:, at:at + n].astype(jnp.float32)
            values = apply_adam_rule(weights[...], first[...], second[...], grads)
            for out, value in zip(outs, values):
                out[...] = value
            outs[3][...] = values[0].astype(jnp.bfloat16)

    operands = [keep, arrived, *in_state, *out_state]
    shapes = []
    for n in (features, columns):
        shapes += [jax.ShapeDtypeStruct((ranks, n), jnp.float32)] * 3 + [jax.ShapeDtypeStruct((ranks, n), jnp.bfloat16)]
    return call(
        body,
        place,
        operands,
        [whole(o.shape) for o in operands],
        earlier,
        shapes,
        [whole(s.shape) for s in shapes],
        moved=32 * ranks * (features + columns),
    )


def inner_products(place, x, near, far, share, earlier):
    rows, ranks = x.shape[0], 2 * near.shape[0]
    sent = rows - share

    def body(place_ref, x_ref, near_ref, far_ref, inner_ref, send_ref):
        half = ranks // 2
        for at, ref in ((0, near_ref), (half, far_ref)):
            inner_ref[:, at:at + half] = lax.dot_general(
                x_ref[...], ref[...], (((1,), (1,)), ((), ())), preferred_element_type=jnp.float32
            )
        send_ref[...] = inner_ref[pl.ds(pl.multiple_of(place_ref[SEND_ROW], share), sent), :]

    return call(
        body,
        place,
        [x, near, far],
        [whole(x.shape), whole(near.shape), whole(far.shape)],
        earlier,
        [jax.ShapeDtypeStruct((rows, ranks), jnp.float32), jax.ShapeDtypeStruct((sent, ranks), jnp.float32)],
        [whole((rows, ranks)), whole((sent, ranks))],
        flops=2 * rows * ranks * x.shape[1],
        moved=2 * rows * x.shape[1],
    )


def spread_inner(place, terms, share, earlier):
    ranks = terms[0].shape[1]
    portion = ranks // 4

    def body(place_ref, own_ref, one_ref, two_ref, three_ref, out_ref):
        inner = factor_scale * own_total((own_ref, one_ref, two_ref, three_ref))
        block = lax.broadcasted_iota(jnp.int32, (ranks, ranks), 1) // portion
        source = jnp.full((ranks, ranks), 0, jnp.int32)
        for i in range(4):
            source = jnp.where(block == i, place_ref[ORDER + i], source)
        column = lax.broadcasted_iota(jnp.int32, (ranks, ranks), 1) % portion
        chosen = lax.broadcasted_iota(jnp.int32, (ranks, ranks), 0) == source * portion + column
        chosen = jnp.where(chosen, 1.0, 0.0).astype(jnp.bfloat16)
        halves = [
            jnp.dot(half, chosen, preferred_element_type=jnp.float32) for half in split_high_low(inner)
        ]
        out_ref[...] = jnp.concatenate(halves, axis=1).astype(jnp.bfloat16)

    return call(
        body,
        place,
        list(terms),
        own_block_specs(share, ranks),
        earlier,
        jax.ShapeDtypeStruct((share, 2 * ranks), jnp.bfloat16),
        whole((share, 2 * ranks)),
    )


def local_line(
    base,
    decoded_row_activations,
    input_factor,
    output_factor,
    input_first_moment,
    input_second_moment,
    output_first_moment,
    output_second_moment,
    replica_input_gradient,
    replica_output_gradient,
):
    x = decoded_row_activations
    width = base.shape[1]
    share = x.shape[0] // 4
    ranks = input_factor.shape[1]
    place = place_numbers(share)
    part_in = replica_input_gradient[0].T.reshape(2, 2, ranks, -1)
    part_out = replica_output_gradient[0].reshape(2, 2, ranks, -1)

    unit = width // sum(CHUNKS)
    widths = [unit * c for c in CHUNKS]
    starts = [sum(widths[:i]) for i in range(len(widths))]
    count = len(widths)
    partials, seconds, thirds, arrived = {}, {}, {}, {}

    def line(step, values):
        return lax.ppermute(values, "tp", LINE[step])

    def chip(bit, values):
        return lax.ppermute(values, "rep", [(i, i ^ bit) for i in range(4)])

    def matmul(c, *earlier):
        most = 256 if c == 0 else 512
        partials[c], send = matmul_chunk(place, x, base, starts[c], widths[c], share, earlier, most)
        arrived[c, 0] = line(0, send)
        return send

    def second(c, *earlier):
        seconds[c] = add_second(place, partials[c], arrived[c, 0], share, earlier)
        arrived[c, 1] = line(1, seconds[c])
        return seconds[c]

    def third(c, *earlier):
        thirds[c] = add_third(place, partials[c], arrived[c, 1], share, earlier)
        arrived[c, 2] = line(2, thirds[c])
        return thirds[c]

    last = matmul(0)
    last = matmul(1, last)
    last = matmul(2, last)
    last = gradients_out(place, part_in, part_out, [last])
    from_core = chip(1, last)
    last = second(0, last)
    last = matmul(3, last)
    across, keep = gradients_on(place, part_in, part_out, from_core, [last])
    from_chip = chip(2, across)
    last = second(1, keep)
    last = third(0, last)
    in_state = (input_factor.T, input_first_moment.T, input_second_moment.T)
    out_state = (output_factor, output_first_moment, output_second_moment)
    states = update_factors(place, keep, from_chip, in_state, out_state, [last])
    new_in, first_in, second_in, half_in, new_out, first_out, second_out, half_out = states
    near_in = jnp.concatenate([half_in, chip(1, half_in)], axis=0)
    far_in = chip(2, near_in)
    turned = lax.ppermute(half_out, ("rep", "tp"), [(4 * a + b, 4 * b + a) for a in range(4) for b in range(4)])
    last = second(2, half_out)
    last = matmul(4, last)
    last = matmul(5, last)
    last = third(1, last)
    inner, inner_send = inner_products(place, x, near_in, far_in, share, [last])
    inner_arrived = [line(0, inner_send)]
    last = third(2, inner_send)
    pair = jnp.concatenate([turned, lax.ppermute(turned, "tp", [(i, i ^ 1) for i in range(4)])], axis=0)
    near_out = line(1, pair)
    inner_second = add_second(place, inner, inner_arrived[0], share, [last])
    inner_arrived.append(line(1, inner_second))
    far_out = line(2, near_out)
    last = second(3, inner_second)
    inner_third = add_third(place, inner, inner_arrived[1], share, [last])
    inner_arrived.append(line(2, inner_third))
    last = second(4, inner_third)
    last = third(3, last)
    spread = spread_inner(place, (inner, *inner_arrived), share, [last])

    decoded = None

    def finish(c, decoded, *earlier):
        terms = (partials[c], arrived[c, 0], arrived[c, 1], arrived[c, 2])
        return finish_chunk(
            place, terms, spread, (pair, near_out, far_out), decoded, starts[c], widths[c], share, width, earlier
        )

    decoded = finish(0, None)
    decoded = finish(1, decoded)
    last = second(5, decoded)
    last = third(4, last)
    decoded = finish(2, decoded, last)
    last = third(5, decoded)
    for c in range(3, count):
        decoded = finish(c, decoded, last)
    return (decoded, new_in.T, new_out, first_in.T, second_in.T, first_out, second_out)


def solution(mesh):
    line = mesh.shape["rep"] == 4 and mesh.shape["tp"] == 4
    return jax.shard_map(
        local_line if line else local_any,
        mesh=mesh,
        in_specs=(
            P("tp", "rep"),
            P("groups", "tp"),
            P(("groups", "tp"), "rep"),
            P("rep", ("groups", "tp")),
            P(("groups", "tp"), "rep"),
            P(("groups", "tp"), "rep"),
            P("rep", ("groups", "tp")),
            P("rep", ("groups", "tp")),
            P("rep", ("groups", "tp"), None),
            P("rep", None, ("groups", "tp")),
        ),
        out_specs=(
            P(("groups", "tp"), "rep"),
            P(("groups", "tp"), "rep"),
            P("rep", ("groups", "tp")),
            P(("groups", "tp"), "rep"),
            P(("groups", "tp"), "rep"),
            P("rep", ("groups", "tp")),
            P("rep", ("groups", "tp")),
        ),
        check_vma=False,
    )
```

```python
import jax
import jax.numpy as jnp
from jax import lax
from jax.experimental import pallas as pl
from jax.experimental.pallas import tpu as pltpu
from jax.sharding import PartitionSpec as P

ADAM_STEP = 200


beta_one = 0.9
beta_two = 0.999
learn_rate = 0.003
adam_eps = 1e-08
factor_scale = 2.0

CHUNKS = ((16, 2), (12, 3), (0, 4), (4, 4), (8, 4), (18, 2), (15, 1))
VMEM_BYTES = 40 * 1024 * 1024
WEIGHT = 5


def apply_adam_rule(weights, moment, second, grads):
    moment_new = beta_one * moment + (1.0 - beta_one) * grads
    second_new = beta_two * second + (1.0 - beta_two) * grads * grads
    first_fix = 1.0 - beta_one**ADAM_STEP
    second_fix = 1.0 - beta_two**ADAM_STEP
    step_size = moment_new / first_fix / (jnp.sqrt(second_new / second_fix) + adam_eps)
    return (weights - learn_rate * step_size, moment_new, second_new)


def scatter_sum_rep(part):
    reps = lax.axis_size("rep")
    me = lax.axis_index("rep")
    share = part.shape[0] // reps
    blocks = part.reshape(reps, share, part.shape[1])
    bit = 1
    while bit < reps:
        pairs = blocks.reshape(blocks.shape[0] // 2, 2, share, part.shape[1])
        mine_bit = (me // bit) % 2
        keep = lax.dynamic_index_in_dim(pairs, mine_bit, 1, keepdims=False)
        send = lax.dynamic_index_in_dim(pairs, 1 - mine_bit, 1, keepdims=False)
        got = lax.ppermute(send.astype(jnp.bfloat16), "rep", [(i, i ^ bit) for i in range(reps)])
        blocks = keep + got.astype(jnp.float32)
        bit *= 2
    return blocks[0]


def split_high_low(values):
    high = values.astype(jnp.bfloat16)
    low = (values - high.astype(jnp.float32)).astype(jnp.bfloat16)
    return high, low


def local_any(
    base,
    decoded_row_activations,
    input_factor,
    output_factor,
    input_first_moment,
    input_second_moment,
    output_first_moment,
    output_second_moment,
    replica_input_gradient,
    replica_output_gradient,
):
    x = decoded_row_activations
    width = base.shape[1]
    features = base.shape[0]
    reps = lax.axis_size("rep")
    part = jnp.concatenate([replica_input_gradient[0].T, replica_output_gradient[0]], axis=1)
    grads = scatter_sum_rep(part)
    grads_in, grads_out = grads[:, :features], grads[:, features:]
    new_in, first_in, second_in = apply_adam_rule(input_factor.T, input_first_moment.T, input_second_moment.T, grads_in)
    new_out, first_out, second_out = apply_adam_rule(output_factor, output_first_moment, output_second_moment, grads_out)
    half_in = new_in.astype(jnp.bfloat16)
    half_out = new_out.astype(jnp.bfloat16)
    inner = lax.dot_general(x, half_in, (((1,), (1,)), ((), ())), preferred_element_type=jnp.float32)
    inner = lax.psum_scatter(inner, "tp", scatter_dimension=0, tiled=True)
    inner = lax.all_gather(inner, "rep", axis=1, tiled=True)
    gathered = lax.all_gather(half_out, ("rep", "tp"), axis=1, tiled=True)
    stacked = gathered.reshape(half_out.shape[0], reps, -1)
    full_out = jnp.transpose(stacked, (1, 0, 2)).reshape(half_out.shape[0] * reps, -1)
    full_out = lax.dynamic_slice_in_dim(full_out, lax.axis_index("rep") * width, width, 1)
    high, low = split_high_low(factor_scale * inner)
    spread = jnp.concatenate([high, low], axis=1)
    doubled = jnp.concatenate([full_out, full_out], axis=0)
    partial = jnp.dot(x, base, preferred_element_type=jnp.float32)
    summed = lax.psum_scatter(partial, "tp", scatter_dimension=0, tiled=True)
    decoded = summed + jnp.dot(spread, doubled, preferred_element_type=jnp.float32)
    return (decoded, new_in.T, new_out, first_in.T, second_in.T, first_out, second_out)


LINE = (((0, 1), (3, 2)), ((1, 2), (2, 1)), ((2, 3), (1, 0)))
(SEND_ROW, SECOND_AT, THIRD_AT, THIRD_FROM, OWN, FIRST_OWN, SECOND_OWN, ORDER, CORE_BIT, CHIP_BIT) = (
    0, 1, 2, 3, 4, 5, 6, 7, 11, 12)
MOST = 2048


def place_numbers(share):
    me, rep = lax.axis_index("tp"), lax.axis_index("rep")
    low = me < 2
    order = [me, me ^ 1, jnp.where(low, 2, 1), jnp.where(low, 3, 0)]
    numbers = [
        jnp.where(me == 0, share, 0),
        jnp.where(me == 1, 1, 0),
        jnp.where(me == 2, 3, 0),
        jnp.where(me == 2, 1, 0),
        me,
        jnp.where(me == 1, 0, 2),
        jnp.where(me == 2, 0, 1),
    ]
    numbers += [rank ^ rep for rank in order] + [rep & 1, rep >> 1]
    return jnp.stack([jnp.asarray(n, jnp.int32) for n in numbers])


def call(body, place, operands, specs, earlier, out_shapes, out_specs, grid=(1,), flops=0, moved=0, scratch=()):
    count = len(operands)

    def kernel(place_ref, *refs):
        body(place_ref, *refs[:count], *refs[count + len(earlier):])

    return pl.pallas_call(
        kernel,
        grid_spec=pltpu.PrefetchScalarGridSpec(
            num_scalar_prefetch=1,
            grid=grid,
            in_specs=list(specs) + [pl.BlockSpec(memory_space=pl.ANY)] * len(earlier),
            out_specs=out_specs,
            scratch_shapes=scratch,
        ),
        out_shape=out_shapes,
        compiler_params=pltpu.CompilerParams(vmem_limit_bytes=VMEM_BYTES),
        cost_estimate=pl.CostEstimate(flops=WEIGHT * flops, bytes_accessed=WEIGHT * moved, transcendentals=0),
    )(place, *operands, *earlier)


def whole(shape):
    return pl.BlockSpec(shape, lambda *_: (0,) * len(shape))


def block_width(start, width, most):
    block = min(most, width)
    while start % block or width % block:
        block //= 2
    return block


def matmul_chunk(place, x, base, start, width, share, earlier, most):
    rows, depth = x.shape
    block = block_width(start, width, most)
    sent = rows - share

    def body(place_ref, x_ref, base_ref, partial_ref, send_ref):
        partial_ref[...] = jnp.dot(x_ref[...], base_ref[...], preferred_element_type=jnp.float32)
        row = pl.multiple_of(place_ref[SEND_ROW], share)
        send_ref[...] = partial_ref[pl.ds(row, sent), :].astype(jnp.bfloat16)

    return call(
        body,
        place,
        [x, base],
        [whole(x.shape), pl.BlockSpec((depth, block), lambda j, p: (0, start // block + j))],
        earlier,
        [jax.ShapeDtypeStruct((rows, width), jnp.float32), jax.ShapeDtypeStruct((sent, width), jnp.bfloat16)],
        [pl.BlockSpec((rows, block), lambda j, p: (0, j)), pl.BlockSpec((sent, block), lambda j, p: (0, j))],
        grid=(width // block,),
        flops=2 * rows * depth * width,
        moved=2 * depth * width,
    )


def add_second(place, partial, arrived, share, earlier):
    width = partial.shape[1]
    block = block_width(0, width, MOST)

    def body(place_ref, partial_ref, upper_ref, lower_ref, out_ref):
        out_ref[:share, :] = (partial_ref[:share, :] + upper_ref[...].astype(jnp.float32)).astype(out_ref.dtype)
        out_ref[share:, :] = (partial_ref[share:, :] + lower_ref[...].astype(jnp.float32)).astype(out_ref.dtype)

    return call(
        body,
        place,
        [partial, arrived, arrived],
        [
            pl.BlockSpec((2 * share, block), lambda j, p: (p[SECOND_AT], j)),
            pl.BlockSpec((share, block), lambda j, p: (p[SECOND_AT], j)),
            pl.BlockSpec((share, block), lambda j, p: (p[SECOND_AT] + 1, j)),
        ],
        earlier,
        jax.ShapeDtypeStruct((2 * share, width), arrived.dtype),
        pl.BlockSpec((2 * share, block), lambda j, p: (0, j)),
        grid=(width // block,),
        moved=16 * share * width,
    )


def add_third(place, partial, arrived, share, earlier):
    width = partial.shape[1]
    block = block_width(0, width, MOST)

    def body(place_ref, partial_ref, arrived_ref, out_ref):
        out_ref[...] = (partial_ref[...] + arrived_ref[...].astype(jnp.float32)).astype(out_ref.dtype)

    return call(
        body,
        place,
        [partial, arrived],
        [
            pl.BlockSpec((share, block), lambda j, p: (p[THIRD_AT], j)),
            pl.BlockSpec((share, block), lambda j, p: (p[THIRD_FROM], j)),
        ],
        earlier,
        jax.ShapeDtypeStruct((share, width), arrived.dtype),
        pl.BlockSpec((share, block), lambda j, p: (0, j)),
        grid=(width // block,),
        moved=8 * share * width,
    )


def own_block_specs(share, block):
    return [
        pl.BlockSpec((share, block), lambda j, p: (p[OWN], j)),
        pl.BlockSpec((share, block), lambda j, p: (p[FIRST_OWN], j)),
        pl.BlockSpec((share, block), lambda j, p: (p[SECOND_OWN], j)),
        pl.BlockSpec((share, block), lambda j, p: (0, j)),
    ]


def own_total(refs):
    total = refs[0][...]
    for ref in refs[1:]:
        total = total + ref[...].astype(jnp.float32)
    return total


def finish_specs(share, block, first, spread, factors):
    half = factors[0].shape[0]
    return own_block_specs(share, block) + [whole(spread.shape)] + [
        pl.BlockSpec((half, block), lambda j, p: (0, first + j))
    ] * 3


def finish_value(refs):
    spread_ref, pair_ref, near_ref, far_ref = refs[4:8]
    other = near_ref[...] + far_ref[...]
    ranks = jnp.concatenate([pair_ref[...], other, pair_ref[...], other], axis=0)
    return own_total(refs[:4]) + jnp.dot(spread_ref[...], ranks, preferred_element_type=jnp.float32)


def finish_chunk(place, terms, spread, factors, start, width, share, earlier):
    block = block_width(start, width, MOST)

    def body(place_ref, *refs):
        refs[-1][...] = finish_value(refs)

    return call(
        body,
        place,
        [*terms, spread, *factors],
        finish_specs(share, block, start // block, spread, factors),
        earlier,
        jax.ShapeDtypeStruct((share, width), jnp.float32),
        pl.BlockSpec((share, block), lambda j, p: (0, j)),
        grid=(width // block,),
        moved=14 * share * width,
    )


def finish_all(place, terms, spread, factors, start, width, share, full_width, done):
    chunks = [chunk for _, chunk in done]

    def body(place_ref, *refs):
        others = refs[8:8 + len(chunks)]
        out_ref, held, semaphores = refs[8 + len(chunks):]
        copies = []
        for i, ((at, chunk), ref) in enumerate(zip(done, others)):
            copies.append(
                pltpu.make_async_copy(ref, out_ref.at[:, at:at + chunk.shape[1]], semaphores.at[i])
            )
        for copy in copies:
            copy.start()
        held[...] = finish_value(refs)
        last = pltpu.make_async_copy(held, out_ref.at[:, start:start + width], semaphores.at[len(chunks)])
        last.start()
        for copy in copies + [last]:
            copy.wait()

    return call(
        body,
        place,
        [*terms, spread, *factors, *chunks],
        finish_specs(share, width, start // width, spread, factors) + [pl.BlockSpec(memory_space=pl.ANY)] * len(chunks),
        [],
        jax.ShapeDtypeStruct((share, full_width), jnp.float32),
        pl.BlockSpec(memory_space=pl.ANY),
        moved=8 * share * full_width,
        scratch=[
            pltpu.VMEM((share, width), jnp.float32),
            pltpu.SemaphoreType.DMA((len(chunks) + 1,)),
        ],
    )


def gradients_out(place, part_in, part_out, earlier):
    features, columns = part_in.shape[3], part_out.shape[3]
    rows = 2 * part_in.shape[2]

    def body(place_ref, in_ref, out_ref, send_ref):
        send_ref[:, :features] = in_ref[...].reshape(rows, features).astype(jnp.bfloat16)
        send_ref[:, features:] = out_ref[...].reshape(rows, columns).astype(jnp.bfloat16)

    shape = (rows, features + columns)
    return call(
        body,
        place,
        [part_in, part_out],
        [
            pl.BlockSpec((2, 1, rows // 2, n), lambda j, p: (0, 1 - p[CORE_BIT], 0, 0))
            for n in (features, columns)
        ],
        earlier,
        jax.ShapeDtypeStruct(shape, jnp.bfloat16),
        whole(shape),
        moved=6 * shape[0] * shape[1],
    )


def gradients_on(place, part_in, part_out, arrived, earlier):
    features, columns = part_in.shape[3], part_out.shape[3]
    ranks = part_in.shape[2]

    def body(place_ref, in_ref, out_ref, arrived_ref, send_ref, keep_ref):
        upper = place_ref[CHIP_BIT] == 0
        for ref, at, n in ((in_ref, 0, features), (out_ref, features, columns)):
            total = ref[...].reshape(2 * ranks, n) + arrived_ref[:, at:at + n].astype(jnp.float32)
            keep_ref[:, at:at + n] = jnp.where(upper, total[:ranks], total[ranks:])
            send_ref[:, at:at + n] = jnp.where(upper, total[ranks:], total[:ranks]).astype(jnp.bfloat16)

    shape = (ranks, features + columns)
    return call(
        body,
        place,
        [part_in, part_out, arrived],
        [pl.BlockSpec((2, 1, ranks, n), lambda j, p: (0, p[CORE_BIT], 0, 0)) for n in (features, columns)]
        + [whole(arrived.shape)],
        earlier,
        [jax.ShapeDtypeStruct(shape, jnp.bfloat16), jax.ShapeDtypeStruct(shape, jnp.float32)],
        [whole(shape)] * 2,
        moved=20 * shape[0] * shape[1],
    )


def update_factors(place, keep, arrived, in_state, out_state, earlier):
    features, columns = in_state[0].shape[1], out_state[0].shape[1]
    ranks = keep.shape[0]

    def body(place_ref, keep_ref, arrived_ref, *refs):
        for side, at, n in ((0, 0, features), (1, features, columns)):
            weights, first, second = refs[3 * side:3 * side + 3]
            outs = refs[6 + 4 * side:10 + 4 * side]
            grads = keep_ref[:, at:at + n] + arrived_ref[:, at:at + n].astype(jnp.float32)
            values = apply_adam_rule(weights[...], first[...], second[...], grads)
            for out, value in zip(outs, values):
                out[...] = value
            outs[3][...] = values[0].astype(jnp.bfloat16)

    operands = [keep, arrived, *in_state, *out_state]
    shapes = []
    for n in (features, columns):
        shapes += [jax.ShapeDtypeStruct((ranks, n), jnp.float32)] * 3 + [jax.ShapeDtypeStruct((ranks, n), jnp.bfloat16)]
    return call(
        body,
        place,
        operands,
        [whole(o.shape) for o in operands],
        earlier,
        shapes,
        [whole(s.shape) for s in shapes],
        moved=32 * ranks * (features + columns),
    )


def join_ranks(place, upper, lower, earlier):
    ranks, width = upper.shape
    block = block_width(0, width, MOST)

    def body(place_ref, upper_ref, lower_ref, out_ref):
        both = [ref[...].astype(jnp.float32) for ref in (upper_ref, lower_ref)]
        out_ref[...] = jnp.concatenate(both, axis=0).astype(jnp.bfloat16)

    return call(
        body,
        place,
        [upper, lower],
        [pl.BlockSpec((ranks, block), lambda j, p: (0, j))] * 2,
        earlier,
        jax.ShapeDtypeStruct((2 * ranks, width), jnp.bfloat16),
        pl.BlockSpec((2 * ranks, block), lambda j, p: (0, j)),
        grid=(width // block,),
        moved=8 * ranks * width,
    )


def inner_products(place, x, near, far, earlier):
    rows, half = x.shape[0], near.shape[0]

    def body(place_ref, x_ref, near_ref, far_ref, inner_ref):
        for at, ref in ((0, near_ref), (half, far_ref)):
            inner_ref[at:at + half, :] = lax.dot_general(
                ref[...], x_ref[...], (((1,), (1,)), ((), ())), preferred_element_type=jnp.float32
            )

    return call(
        body,
        place,
        [x, near, far],
        [whole(x.shape), whole(near.shape), whole(far.shape)],
        earlier,
        jax.ShapeDtypeStruct((2 * half, rows), jnp.float32),
        whole((2 * half, rows)),
        flops=4 * rows * half * x.shape[1],
        moved=2 * rows * x.shape[1],
    )


def inner_sum(place, inner, arrived, earlier):
    def body(place_ref, inner_ref, arrived_ref, out_ref):
        out_ref[...] = inner_ref[...] + arrived_ref[...]

    return call(
        body,
        place,
        [inner, arrived],
        [whole(inner.shape)] * 2,
        earlier,
        jax.ShapeDtypeStruct(inner.shape, jnp.float32),
        whole(inner.shape),
    )


def spread_inner(place, inner, arrived, share, earlier):
    ranks, rows = inner.shape
    portion = ranks // 4

    def body(place_ref, inner_ref, arrived_ref, out_ref):
        total = factor_scale * (inner_ref[...] + arrived_ref[...])
        shape = (share, rows)
        mine = lax.broadcasted_iota(jnp.int32, shape, 0) + place_ref[OWN] * share
        mine = jnp.where(lax.broadcasted_iota(jnp.int32, shape, 1) == mine, 1.0, 0.0).astype(jnp.bfloat16)
        block = lax.broadcasted_iota(jnp.int32, (ranks, ranks), 1) // portion
        source = jnp.full((ranks, ranks), 0, jnp.int32)
        for i in range(4):
            source = jnp.where(block == i, place_ref[ORDER + i], source)
        column = lax.broadcasted_iota(jnp.int32, (ranks, ranks), 1) % portion
        chosen = lax.broadcasted_iota(jnp.int32, (ranks, ranks), 0) == source * portion + column
        chosen = jnp.where(chosen, 1.0, 0.0).astype(jnp.bfloat16)
        halves = []
        for half in split_high_low(total):
            turned = lax.dot_general(mine, half, (((1,), (1,)), ((), ())), preferred_element_type=jnp.float32)
            halves.append(jnp.dot(turned.astype(jnp.bfloat16), chosen, preferred_element_type=jnp.float32))
        out_ref[...] = jnp.concatenate(halves, axis=1).astype(jnp.bfloat16)

    return call(
        body,
        place,
        [inner, arrived],
        [whole(inner.shape)] * 2,
        earlier,
        jax.ShapeDtypeStruct((share, 2 * ranks), jnp.bfloat16),
        whole((share, 2 * ranks)),
    )


def local_line(
    base,
    decoded_row_activations,
    input_factor,
    output_factor,
    input_first_moment,
    input_second_moment,
    output_first_moment,
    output_second_moment,
    replica_input_gradient,
    replica_output_gradient,
):
    x = decoded_row_activations
    width = base.shape[1]
    share = x.shape[0] // 4
    ranks = input_factor.shape[1]
    place = place_numbers(share)
    part_in = replica_input_gradient[0].T.reshape(2, 2, ranks, -1)
    part_out = replica_output_gradient[0].reshape(2, 2, ranks, -1)

    unit = width // 20
    starts = [unit * at for at, _ in CHUNKS]
    widths = [unit * wide for _, wide in CHUNKS]
    partials, seconds, thirds, arrived = {}, {}, {}, {}

    def line(step, values):
        return lax.ppermute(values, "tp", LINE[step])

    def chip(bit, values):
        return lax.ppermute(values, "rep", [(i, i ^ bit) for i in range(4)])

    def matmul(c, *earlier):
        partials[c], send = matmul_chunk(place, x, base, starts[c], widths[c], share, earlier, 512)
        arrived[c, 0] = line(0, send)
        return send

    def second(c, *earlier):
        seconds[c] = add_second(place, partials[c], arrived[c, 0], share, earlier)
        arrived[c, 1] = line(1, seconds[c])
        return seconds[c]

    def third(c, *earlier):
        thirds[c] = add_third(place, partials[c], arrived[c, 1], share, earlier)
        arrived[c, 2] = line(2, thirds[c])
        return thirds[c]

    def terms(c):
        return (partials[c], arrived[c, 0], arrived[c, 1], arrived[c, 2])

    def finish(c, *earlier):
        finished.append((starts[c], finish_chunk(
            place, terms(c), spread, (pair, near_out, far_out), starts[c], widths[c], share, earlier
        )))
        return finished[-1][1]

    finished = []
    last = matmul(0)
    last = gradients_out(place, part_in, part_out, [last])
    from_core = chip(1, last)
    last = matmul(1, last)
    across, last = gradients_on(place, part_in, part_out, from_core, [last])
    keep = last
    from_chip = chip(2, across)
    last = matmul(2, last)
    last = second(0, last)
    in_state = (input_factor.T, input_first_moment.T, input_second_moment.T)
    out_state = (output_factor, output_first_moment, output_second_moment)
    states = update_factors(place, keep, from_chip, in_state, out_state, [last])
    new_in, first_in, second_in, half_in, new_out, first_out, second_out, half_out = states
    turned = lax.ppermute(half_out, ("rep", "tp"), [(4 * a + b, 4 * b + a) for a in range(4) for b in range(4)])
    near_in = jnp.concatenate([half_in, chip(1, half_in)], axis=0)
    far_in = chip(2, near_in)
    last = matmul(3, half_out)
    last = second(1, last)
    last = third(0, last, turned)
    swapped = lax.ppermute(turned, "tp", [(i, i ^ 1) for i in range(4)])
    last = second(2, last)
    last = matmul(4, last)
    last = inner = inner_products(place, x, near_in, far_in, [last])
    inner_arrived = lax.ppermute(inner, "tp", [(i, i ^ 1) for i in range(4)])
    last = third(1, last)
    last = second(3, last)
    last = matmul(5, last)
    last = pair = join_ranks(place, turned, swapped, [last])
    near_out = line(1, pair)
    last = inner = inner_sum(place, inner, inner_arrived, [last])
    inner_arrived = lax.ppermute(inner, "tp", [(i, i ^ 2) for i in range(4)])
    last = third(2, last)
    last = matmul(6, last)
    last = second(4, last)
    last = third(3, last)
    last = spread = spread_inner(place, inner, inner_arrived, share, [last, near_out])
    far_out = line(2, near_out)
    last = second(5, last)
    last = finish(0, last, far_out)
    last = finish(1, last)
    last = third(4, last)
    last = second(6, last)
    last = third(5, last)
    last = finish(2, last)
    last = finish(3, last)
    last = third(6, last)
    last = finish(4, last)
    last = finish(5, last)
    decoded = finish_all(
        place, terms(6), spread, (pair, near_out, far_out), starts[6], widths[6], share, width, finished
    )
    return (decoded, new_in.T, new_out, first_in.T, second_in.T, first_out, second_out)


def solution(mesh):
    line = mesh.shape["rep"] == 4 and mesh.shape["tp"] == 4
    return jax.shard_map(
        local_line if line else local_any,
        mesh=mesh,
        in_specs=(
            P("tp", "rep"),
            P("groups", "tp"),
            P(("groups", "tp"), "rep"),
            P("rep", ("groups", "tp")),
            P(("groups", "tp"), "rep"),
            P(("groups", "tp"), "rep"),
            P("rep", ("groups", "tp")),
            P("rep", ("groups", "tp")),
            P("rep", ("groups", "tp"), None),
            P("rep", None, ("groups", "tp")),
        ),
        out_specs=(
            P(("groups", "tp"), "rep"),
            P(("groups", "tp"), "rep"),
            P("rep", ("groups", "tp")),
            P(("groups", "tp"), "rep"),
            P(("groups", "tp"), "rep"),
            P("rep", ("groups", "tp")),
            P("rep", ("groups", "tp")),
        ),
        check_vma=False,
    )
```

```python
import jax
import jax.numpy as jnp
from jax import lax
from jax.experimental import pallas as pl
from jax.experimental.pallas import tpu as pltpu
from jax.sharding import PartitionSpec as P

ADAM_STEP = 200


beta_one = 0.9
beta_two = 0.999
learn_rate = 0.003
adam_eps = 1e-08
factor_scale = 2.0

CHUNKS = ((16, 2), (12, 3), (0, 4), (4, 4), (8, 4), (18, 2), (15, 1))
VMEM_BYTES = 40 * 1024 * 1024
WEIGHT = 5


def apply_adam_rule(weights, moment, second, grads):
    moment_new = beta_one * moment + (1.0 - beta_one) * grads
    second_new = beta_two * second + (1.0 - beta_two) * grads * grads
    first_fix = 1.0 - beta_one**ADAM_STEP
    second_fix = 1.0 - beta_two**ADAM_STEP
    step_size = moment_new / first_fix / (jnp.sqrt(second_new / second_fix) + adam_eps)
    return (weights - learn_rate * step_size, moment_new, second_new)


def scatter_sum_rep(part):
    reps = lax.axis_size("rep")
    me = lax.axis_index("rep")
    share = part.shape[0] // reps
    blocks = part.reshape(reps, share, part.shape[1])
    bit = 1
    while bit < reps:
        pairs = blocks.reshape(blocks.shape[0] // 2, 2, share, part.shape[1])
        mine_bit = (me // bit) % 2
        keep = lax.dynamic_index_in_dim(pairs, mine_bit, 1, keepdims=False)
        send = lax.dynamic_index_in_dim(pairs, 1 - mine_bit, 1, keepdims=False)
        got = lax.ppermute(send.astype(jnp.bfloat16), "rep", [(i, i ^ bit) for i in range(reps)])
        blocks = keep + got.astype(jnp.float32)
        bit *= 2
    return blocks[0]


def split_high_low(values):
    high = values.astype(jnp.bfloat16)
    low = (values - high.astype(jnp.float32)).astype(jnp.bfloat16)
    return high, low


def local_any(
    base,
    decoded_row_activations,
    input_factor,
    output_factor,
    input_first_moment,
    input_second_moment,
    output_first_moment,
    output_second_moment,
    replica_input_gradient,
    replica_output_gradient,
):
    x = decoded_row_activations
    width = base.shape[1]
    features = base.shape[0]
    reps = lax.axis_size("rep")
    part = jnp.concatenate([replica_input_gradient[0].T, replica_output_gradient[0]], axis=1)
    grads = scatter_sum_rep(part)
    grads_in, grads_out = grads[:, :features], grads[:, features:]
    new_in, first_in, second_in = apply_adam_rule(input_factor.T, input_first_moment.T, input_second_moment.T, grads_in)
    new_out, first_out, second_out = apply_adam_rule(output_factor, output_first_moment, output_second_moment, grads_out)
    half_in = new_in.astype(jnp.bfloat16)
    half_out = new_out.astype(jnp.bfloat16)
    inner = lax.dot_general(x, half_in, (((1,), (1,)), ((), ())), preferred_element_type=jnp.float32)
    inner = lax.psum_scatter(inner, "tp", scatter_dimension=0, tiled=True)
    inner = lax.all_gather(inner, "rep", axis=1, tiled=True)
    gathered = lax.all_gather(half_out, ("rep", "tp"), axis=1, tiled=True)
    stacked = gathered.reshape(half_out.shape[0], reps, -1)
    full_out = jnp.transpose(stacked, (1, 0, 2)).reshape(half_out.shape[0] * reps, -1)
    full_out = lax.dynamic_slice_in_dim(full_out, lax.axis_index("rep") * width, width, 1)
    high, low = split_high_low(factor_scale * inner)
    spread = jnp.concatenate([high, low], axis=1)
    doubled = jnp.concatenate([full_out, full_out], axis=0)
    partial = jnp.dot(x, base, preferred_element_type=jnp.float32)
    summed = lax.psum_scatter(partial, "tp", scatter_dimension=0, tiled=True)
    decoded = summed + jnp.dot(spread, doubled, preferred_element_type=jnp.float32)
    return (decoded, new_in.T, new_out, first_in.T, second_in.T, first_out, second_out)


LINE = (((0, 1), (3, 2)), ((1, 2), (2, 1)), ((2, 3), (1, 0)))
(SEND_ROW, SECOND_AT, THIRD_AT, THIRD_FROM, OWN, FIRST_OWN, SECOND_OWN, ORDER, CORE_BIT, CHIP_BIT) = (
    0, 1, 2, 3, 4, 5, 6, 7, 11, 12)
MOST = 2048


def place_numbers(share):
    me, rep = lax.axis_index("tp"), lax.axis_index("rep")
    low = me < 2
    order = [me, me ^ 1, jnp.where(low, 2, 1), jnp.where(low, 3, 0)]
    numbers = [
        jnp.where(me == 0, share, 0),
        jnp.where(me == 1, 1, 0),
        jnp.where(me == 2, 3, 0),
        jnp.where(me == 2, 1, 0),
        me,
        jnp.where(me == 1, 0, 2),
        jnp.where(me == 2, 0, 1),
    ]
    numbers += [rank ^ rep for rank in order] + [rep & 1, rep >> 1]
    return jnp.stack([jnp.asarray(n, jnp.int32) for n in numbers])


def call(body, place, operands, specs, earlier, out_shapes, out_specs, grid=(1,), flops=0, moved=0):
    count = len(operands)

    def kernel(place_ref, *refs):
        body(place_ref, *refs[:count], *refs[count + len(earlier):])

    return pl.pallas_call(
        kernel,
        grid_spec=pltpu.PrefetchScalarGridSpec(
            num_scalar_prefetch=1,
            grid=grid,
            in_specs=list(specs) + [pl.BlockSpec(memory_space=pl.ANY)] * len(earlier),
            out_specs=out_specs,
        ),
        out_shape=out_shapes,
        compiler_params=pltpu.CompilerParams(vmem_limit_bytes=VMEM_BYTES),
        cost_estimate=pl.CostEstimate(flops=WEIGHT * flops, bytes_accessed=WEIGHT * moved, transcendentals=0),
    )(place, *operands, *earlier)


def whole(shape):
    return pl.BlockSpec(shape, lambda *_: (0,) * len(shape))


def block_width(start, width, most):
    block = min(most, width)
    while start % block or width % block:
        block //= 2
    return block


def matmul_chunk(place, x, base, start, width, share, earlier, most):
    rows, depth = x.shape
    block = block_width(start, width, most)
    sent = rows - share

    def body(place_ref, x_ref, base_ref, partial_ref, send_ref):
        partial_ref[...] = jnp.dot(x_ref[...], base_ref[...], preferred_element_type=jnp.float32)
        row = pl.multiple_of(place_ref[SEND_ROW], share)
        send_ref[...] = partial_ref[pl.ds(row, sent), :].astype(jnp.bfloat16)

    return call(
        body,
        place,
        [x, base],
        [whole(x.shape), pl.BlockSpec((depth, block), lambda j, p: (0, start // block + j))],
        earlier,
        [jax.ShapeDtypeStruct((rows, width), jnp.float32), jax.ShapeDtypeStruct((sent, width), jnp.bfloat16)],
        [pl.BlockSpec((rows, block), lambda j, p: (0, j)), pl.BlockSpec((sent, block), lambda j, p: (0, j))],
        grid=(width // block,),
        flops=2 * rows * depth * width,
        moved=2 * depth * width,
    )


def add_second(place, pieces, share, earlier):
    operands, specs = [], []
    for partial, arrived in pieces:
        width = partial.shape[1]
        operands += [partial, arrived, arrived]
        specs += [
            pl.BlockSpec((2 * share, width), lambda j, p: (p[SECOND_AT], 0)),
            pl.BlockSpec((share, width), lambda j, p: (p[SECOND_AT], 0)),
            pl.BlockSpec((share, width), lambda j, p: (p[SECOND_AT] + 1, 0)),
        ]
    widths = [partial.shape[1] for partial, _ in pieces]

    def body(place_ref, *refs):
        out_ref, at = refs[-1], 0
        for i, width in enumerate(widths):
            partial_ref, upper_ref, lower_ref = refs[3 * i:3 * i + 3]
            to = slice(at, at + width)
            out_ref[:share, to] = (partial_ref[:share, :] + upper_ref[...].astype(jnp.float32)).astype(jnp.bfloat16)
            out_ref[share:, to] = (partial_ref[share:, :] + lower_ref[...].astype(jnp.float32)).astype(jnp.bfloat16)
            at += width

    shape = (2 * share, sum(widths))
    return call(
        body, place, operands, specs, earlier, jax.ShapeDtypeStruct(shape, jnp.bfloat16), whole(shape),
        moved=16 * share * shape[1],
    )


def add_third(place, pieces, share, earlier):
    operands, specs = [], []
    for partial, arrived, _ in pieces:
        operands += [partial, arrived]
        specs += [
            pl.BlockSpec((share, partial.shape[1]), lambda j, p: (p[THIRD_AT], 0)),
            pl.BlockSpec((share, arrived.shape[1]), lambda j, p: (p[THIRD_FROM], 0)),
        ]
    widths = [partial.shape[1] for partial, _, _ in pieces]
    inside = [at for _, _, at in pieces]

    def body(place_ref, *refs):
        out_ref, at = refs[-1], 0
        for i, width in enumerate(widths):
            partial_ref, arrived_ref = refs[2 * i:2 * i + 2]
            arrived = arrived_ref[:, inside[i]:inside[i] + width].astype(jnp.float32)
            out_ref[:, at:at + width] = (partial_ref[...] + arrived).astype(jnp.bfloat16)
            at += width

    shape = (share, sum(widths))
    return call(
        body, place, operands, specs, earlier, jax.ShapeDtypeStruct(shape, jnp.bfloat16), whole(shape),
        moved=8 * share * shape[1],
    )


def finish_chunks(place, pieces, spread, factors, share, earlier, full_width=None, done=()):
    operands, specs = [spread], [whole(spread.shape)]
    half = factors[0].shape[0]
    for start, partial, first, second, _, third, _ in pieces:
        width = partial.shape[1]
        operands += [partial, first, second, third, *factors]
        specs += [
            pl.BlockSpec((share, width), lambda j, p: (p[OWN], 0)),
            pl.BlockSpec((share, width), lambda j, p: (p[FIRST_OWN], 0)),
            pl.BlockSpec((share, second.shape[1]), lambda j, p: (p[SECOND_OWN], 0)),
            whole(third.shape),
        ] + [pl.BlockSpec((half, width), lambda j, p, at=start // width: (0, at))] * 3
    for columns, _ in done:
        operands.append(columns)
        specs.append(whole(columns.shape))
    places = [(start, partial.shape[1], two, three) for start, partial, _, _, two, _, three in pieces]
    shape = (share, sum(width for _, width, _, _ in places) if full_width is None else full_width)

    def body(place_ref, spread_ref, *refs):
        out_ref, at = refs[-1], 0
        for i, (start, width, two, three) in enumerate(places):
            own_ref, first_ref, second_ref, third_ref, pair_ref, near_ref, far_ref = refs[7 * i:7 * i + 7]
            other = near_ref[...] + far_ref[...]
            ranks = jnp.concatenate([pair_ref[...], other, pair_ref[...], other], axis=0)
            total = own_ref[...] + first_ref[...].astype(jnp.float32)
            total = total + second_ref[:, two:two + width].astype(jnp.float32)
            total = total + third_ref[:, three:three + width].astype(jnp.float32)
            total = total + jnp.dot(spread_ref[...], ranks, preferred_element_type=jnp.float32)
            to = at if full_width is None else start
            out_ref[:, to:to + width] = total
            at += width
        for ref, (_, parts) in zip(refs[7 * len(places):], done):
            at = 0
            for start, width in parts:
                out_ref[:, start:start + width] = ref[:, at:at + width]
                at += width

    return call(
        body, place, operands, specs, earlier, jax.ShapeDtypeStruct(shape, jnp.float32), whole(shape),
        moved=14 * share * shape[1],
    )


def gradients_out(place, part_in, part_out, earlier):
    features, columns = part_in.shape[3], part_out.shape[3]
    rows = 2 * part_in.shape[2]

    def body(place_ref, in_ref, out_ref, send_ref):
        send_ref[:, :features] = in_ref[...].reshape(rows, features).astype(jnp.bfloat16)
        send_ref[:, features:] = out_ref[...].reshape(rows, columns).astype(jnp.bfloat16)

    shape = (rows, features + columns)
    return call(
        body,
        place,
        [part_in, part_out],
        [
            pl.BlockSpec((2, 1, rows // 2, n), lambda j, p: (0, 1 - p[CORE_BIT], 0, 0))
            for n in (features, columns)
        ],
        earlier,
        jax.ShapeDtypeStruct(shape, jnp.bfloat16),
        whole(shape),
        moved=6 * shape[0] * shape[1],
    )


def gradients_on(place, part_in, part_out, arrived, earlier):
    features, columns = part_in.shape[3], part_out.shape[3]
    ranks = part_in.shape[2]

    def body(place_ref, in_ref, out_ref, arrived_ref, send_ref, keep_ref):
        upper = place_ref[CHIP_BIT] == 0
        for ref, at, n in ((in_ref, 0, features), (out_ref, features, columns)):
            total = ref[...].reshape(2 * ranks, n) + arrived_ref[:, at:at + n].astype(jnp.float32)
            keep_ref[:, at:at + n] = jnp.where(upper, total[:ranks], total[ranks:])
            send_ref[:, at:at + n] = jnp.where(upper, total[ranks:], total[:ranks]).astype(jnp.bfloat16)

    shape = (ranks, features + columns)
    return call(
        body,
        place,
        [part_in, part_out, arrived],
        [pl.BlockSpec((2, 1, ranks, n), lambda j, p: (0, p[CORE_BIT], 0, 0)) for n in (features, columns)]
        + [whole(arrived.shape)],
        earlier,
        [jax.ShapeDtypeStruct(shape, jnp.bfloat16), jax.ShapeDtypeStruct(shape, jnp.float32)],
        [whole(shape)] * 2,
        moved=20 * shape[0] * shape[1],
    )


def update_factors(place, keep, arrived, in_state, out_state, earlier):
    features, columns = in_state[0].shape[1], out_state[0].shape[1]
    ranks = keep.shape[0]

    def body(place_ref, keep_ref, arrived_ref, *refs):
        for side, at, n in ((0, 0, features), (1, features, columns)):
            weights, first, second = refs[3 * side:3 * side + 3]
            outs = refs[6 + 4 * side:10 + 4 * side]
            grads = keep_ref[:, at:at + n] + arrived_ref[:, at:at + n].astype(jnp.float32)
            values = apply_adam_rule(weights[...], first[...], second[...], grads)
            for out, value in zip(outs, values):
                out[...] = value
            outs[3][...] = values[0].astype(jnp.bfloat16)

    operands = [keep, arrived, *in_state, *out_state]
    shapes = []
    for n in (features, columns):
        shapes += [jax.ShapeDtypeStruct((ranks, n), jnp.float32)] * 3 + [jax.ShapeDtypeStruct((ranks, n), jnp.bfloat16)]
    return call(
        body,
        place,
        operands,
        [whole(o.shape) for o in operands],
        earlier,
        shapes,
        [whole(s.shape) for s in shapes],
        moved=32 * ranks * (features + columns),
    )


def inner_products(place, x, near, far, turned, earlier):
    rows, ranks = x.shape[0], turned.shape[0]
    width = turned.shape[1]
    inner_width = 4 * rows

    def body(place_ref, x_ref, near_ref, far_ref, turned_ref, inner_ref, send_ref):
        for i, ref in enumerate((near_ref, far_ref)):
            products = lax.dot_general(
                ref[...], x_ref[...], (((1,), (1,)), ((), ())), preferred_element_type=jnp.float32
            )
            for j in range(2):
                at = (2 * i + j) * rows
                inner_ref[:, at:at + rows] = products[j * ranks:(j + 1) * ranks]
        high, low = split_high_low(inner_ref[...])
        send_ref[:, :width] = turned_ref[...]
        send_ref[:, width:width + inner_width] = high
        send_ref[:, width + inner_width:] = low

    shapes = [(ranks, inner_width), (ranks, width + 2 * inner_width)]
    return call(
        body,
        place,
        [x, near, far, turned],
        [whole(x.shape), whole(near.shape), whole(far.shape), whole(turned.shape)],
        earlier,
        [jax.ShapeDtypeStruct(shapes[0], jnp.float32), jax.ShapeDtypeStruct(shapes[1], jnp.bfloat16)],
        [whole(shape) for shape in shapes],
        flops=8 * rows * ranks * x.shape[1],
        moved=2 * rows * x.shape[1],
    )


def join_pair(place, turned, swapped, inner, earlier):
    ranks, width = turned.shape
    inner_width = inner.shape[1]

    def body(place_ref, turned_ref, swapped_ref, inner_ref, pair_ref, sum_ref):
        both = [turned_ref[...].astype(jnp.float32), swapped_ref[:, :width].astype(jnp.float32)]
        pair_ref[:, :width] = jnp.concatenate(both, axis=0).astype(jnp.bfloat16)
        total = inner_ref[...] + swapped_ref[:, width:width + inner_width].astype(jnp.float32)
        total = total + swapped_ref[:, width + inner_width:].astype(jnp.float32)
        sum_ref[...] = total
        halves = [half.astype(jnp.float32) for half in split_high_low(total)]
        pair_ref[:, width:] = jnp.concatenate(halves, axis=0).astype(jnp.bfloat16)

    shapes = [(2 * ranks, width + inner_width), (ranks, inner_width)]
    return call(
        body,
        place,
        [turned, swapped, inner],
        [whole(turned.shape), whole(swapped.shape), whole(inner.shape)],
        earlier,
        [jax.ShapeDtypeStruct(shapes[0], jnp.bfloat16), jax.ShapeDtypeStruct(shapes[1], jnp.float32)],
        [whole(shape) for shape in shapes],
        moved=8 * ranks * width,
    )


def spread_inner(place, inner, near, far, width, share, earlier):
    portion = inner.shape[0]
    rows = inner.shape[1] // 4
    ranks = 4 * portion

    def body(place_ref, inner_ref, near_ref, far_ref, out_ref):
        other = near_ref[:, width:].astype(jnp.float32) + far_ref[:, width:].astype(jnp.float32)
        total = factor_scale * (inner_ref[...] + (other[:portion] + other[portion:]))
        total = jnp.concatenate([total[:, i * rows:(i + 1) * rows] for i in range(4)], axis=0)
        shape = (share, rows)
        mine = lax.broadcasted_iota(jnp.int32, shape, 0) + place_ref[OWN] * share
        mine = jnp.where(lax.broadcasted_iota(jnp.int32, shape, 1) == mine, 1.0, 0.0).astype(jnp.bfloat16)
        block = lax.broadcasted_iota(jnp.int32, (ranks, ranks), 1) // portion
        source = jnp.full((ranks, ranks), 0, jnp.int32)
        for i in range(4):
            source = jnp.where(block == i, place_ref[ORDER + i], source)
        column = lax.broadcasted_iota(jnp.int32, (ranks, ranks), 1) % portion
        chosen = lax.broadcasted_iota(jnp.int32, (ranks, ranks), 0) == source * portion + column
        chosen = jnp.where(chosen, 1.0, 0.0).astype(jnp.bfloat16)
        halves = []
        for half in split_high_low(total):
            turned = lax.dot_general(mine, half, (((1,), (1,)), ((), ())), preferred_element_type=jnp.float32)
            halves.append(jnp.dot(turned.astype(jnp.bfloat16), chosen, preferred_element_type=jnp.float32))
        out_ref[...] = jnp.concatenate(halves, axis=1).astype(jnp.bfloat16)

    return call(
        body,
        place,
        [inner, near, far],
        [whole(inner.shape), whole(near.shape), whole(far.shape)],
        earlier,
        jax.ShapeDtypeStruct((share, 2 * ranks), jnp.bfloat16),
        whole((share, 2 * ranks)),
    )


def local_line(
    base,
    decoded_row_activations,
    input_factor,
    output_factor,
    input_first_moment,
    input_second_moment,
    output_first_moment,
    output_second_moment,
    replica_input_gradient,
    replica_output_gradient,
):
    x = decoded_row_activations
    width = base.shape[1]
    share = x.shape[0] // 4
    ranks = input_factor.shape[1]
    place = place_numbers(share)
    part_in = replica_input_gradient[0].T.reshape(2, 2, ranks, -1)
    part_out = replica_output_gradient[0].reshape(2, 2, ranks, -1)

    unit = width // 20
    starts = [unit * at for at, _ in CHUNKS]
    widths = [unit * wide for _, wide in CHUNKS]
    partials, firsts, seconds, thirds = {}, {}, {}, {}

    def line(step, values):
        return lax.ppermute(values, "tp", LINE[step])

    def chip(bit, values):
        return lax.ppermute(values, "rep", [(i, i ^ bit) for i in range(4)])

    def matmul(c, *earlier):
        partials[c], send = matmul_chunk(place, x, base, starts[c], widths[c], share, earlier, 512)
        firsts[c] = line(0, send)
        return send

    def second(chunks, *earlier):
        send = add_second(place, [(partials[c], firsts[c]) for c in chunks], share, earlier)
        got, at = line(1, send), 0
        for c in chunks:
            seconds[c] = (got, at)
            at += widths[c]
        return send

    def third(chunks, *earlier):
        send = add_third(place, [(partials[c], *seconds[c]) for c in chunks], share, earlier)
        got, at = line(2, send), 0
        for c in chunks:
            thirds[c] = (got, at)
            at += widths[c]
        return send

    def finish(chunks, *earlier, full_width=None, done=()):
        pieces = [(starts[c], partials[c], firsts[c], *seconds[c], *thirds[c]) for c in chunks]
        columns = finish_chunks(place, pieces, spread, factors, share, earlier, full_width, done)
        finished.append((columns, [(starts[c], widths[c]) for c in chunks]))
        return columns

    finished = []
    last = matmul(0)
    last = gradients_out(place, part_in, part_out, [last])
    from_core = chip(1, last)
    last = matmul(1, last)
    across, keep = gradients_on(place, part_in, part_out, from_core, [last])
    from_chip = chip(2, across)
    last = matmul(2, keep)
    in_state = (input_factor.T, input_first_moment.T, input_second_moment.T)
    out_state = (output_factor, output_first_moment, output_second_moment)
    states = update_factors(place, keep, from_chip, in_state, out_state, [last])
    new_in, first_in, second_in, half_in, new_out, first_out, second_out, half_out = states
    turned = lax.ppermute(half_out, ("rep", "tp"), [(4 * a + b, 4 * b + a) for a in range(4) for b in range(4)])
    near_in = jnp.concatenate([half_in, chip(1, half_in)], axis=0)
    far_in = chip(2, near_in)
    last = second((0, 1), half_out)
    last = matmul(3, last)
    inner, last = inner_products(place, x, near_in, far_in, turned, [last])
    swapped = lax.ppermute(last, "tp", [(i, i ^ 1) for i in range(4)])
    last = second((2,), last)
    last = matmul(4, last)
    last = second((3,), last)
    last = third((0, 1), last)
    pair, inner = join_pair(place, turned, swapped, inner, [last])
    near_out = line(1, pair)
    last = matmul(5, pair)
    last = matmul(6, last, thirds[0][0])
    last = second((4,), last)
    last = third((2, 3), last)
    far_out = line(2, near_out)
    factors = (pair, near_out, far_out)
    last = second((5,), last)
    last = second((6,), last)
    last = spread = spread_inner(place, inner, near_out, far_out, width, share, [last])
    last = finish((0, 1), last)
    last = third((4,), last)
    last = third((5,), last)
    last = third((6,), last)
    last = finish((2, 3), last)
    last = finish((4,), last)
    last = finish((5,), last)
    decoded = finish((6,), last, full_width=width, done=list(finished))
    return (decoded, new_in.T, new_out, first_in.T, second_in.T, first_out, second_out)


def solution(mesh):
    line = mesh.shape["rep"] == 4 and mesh.shape["tp"] == 4
    return jax.shard_map(
        local_line if line else local_any,
        mesh=mesh,
        in_specs=(
            P("tp", "rep"),
            P("groups", "tp"),
            P(("groups", "tp"), "rep"),
            P("rep", ("groups", "tp")),
            P(("groups", "tp"), "rep"),
            P(("groups", "tp"), "rep"),
            P("rep", ("groups", "tp")),
            P("rep", ("groups", "tp")),
            P("rep", ("groups", "tp"), None),
            P("rep", None, ("groups", "tp")),
        ),
        out_specs=(
            P(("groups", "tp"), "rep"),
            P(("groups", "tp"), "rep"),
            P("rep", ("groups", "tp")),
            P(("groups", "tp"), "rep"),
            P(("groups", "tp"), "rep"),
            P("rep", ("groups", "tp")),
            P("rep", ("groups", "tp")),
        ),
        check_vma=False,
    )
```

```python
import jax
import jax.numpy as jnp
from jax import lax
from jax.experimental import pallas as pl
from jax.experimental.pallas import tpu as pltpu
from jax.sharding import PartitionSpec as P

ADAM_STEP = 200


beta_one = 0.9
beta_two = 0.999
learn_rate = 0.003
adam_eps = 1e-08
factor_scale = 2.0

CHUNKS = ((16, 2), (12, 3), (0, 4), (4, 4), (8, 4), (18, 2), (15, 1))
VMEM_BYTES = 40 * 1024 * 1024
WEIGHT = 5


def apply_adam_rule(weights, moment, second, grads):
    moment_new = beta_one * moment + (1.0 - beta_one) * grads
    second_new = beta_two * second + (1.0 - beta_two) * grads * grads
    first_fix = 1.0 - beta_one**ADAM_STEP
    second_fix = 1.0 - beta_two**ADAM_STEP
    step_size = moment_new / first_fix / (jnp.sqrt(second_new / second_fix) + adam_eps)
    return (weights - learn_rate * step_size, moment_new, second_new)


def scatter_sum_rep(part):
    reps = lax.axis_size("rep")
    me = lax.axis_index("rep")
    share = part.shape[0] // reps
    blocks = part.reshape(reps, share, part.shape[1])
    bit = 1
    while bit < reps:
        pairs = blocks.reshape(blocks.shape[0] // 2, 2, share, part.shape[1])
        mine_bit = (me // bit) % 2
        keep = lax.dynamic_index_in_dim(pairs, mine_bit, 1, keepdims=False)
        send = lax.dynamic_index_in_dim(pairs, 1 - mine_bit, 1, keepdims=False)
        got = lax.ppermute(send.astype(jnp.bfloat16), "rep", [(i, i ^ bit) for i in range(reps)])
        blocks = keep + got.astype(jnp.float32)
        bit *= 2
    return blocks[0]


def split_high_low(values):
    high = values.astype(jnp.bfloat16)
    low = (values - high.astype(jnp.float32)).astype(jnp.bfloat16)
    return high, low


def local_any(
    base,
    decoded_row_activations,
    input_factor,
    output_factor,
    input_first_moment,
    input_second_moment,
    output_first_moment,
    output_second_moment,
    replica_input_gradient,
    replica_output_gradient,
):
    x = decoded_row_activations
    width = base.shape[1]
    features = base.shape[0]
    reps = lax.axis_size("rep")
    part = jnp.concatenate([replica_input_gradient[0].T, replica_output_gradient[0]], axis=1)
    grads = scatter_sum_rep(part)
    grads_in, grads_out = grads[:, :features], grads[:, features:]
    new_in, first_in, second_in = apply_adam_rule(input_factor.T, input_first_moment.T, input_second_moment.T, grads_in)
    new_out, first_out, second_out = apply_adam_rule(output_factor, output_first_moment, output_second_moment, grads_out)
    half_in = new_in.astype(jnp.bfloat16)
    half_out = new_out.astype(jnp.bfloat16)
    inner = lax.dot_general(x, half_in, (((1,), (1,)), ((), ())), preferred_element_type=jnp.float32)
    inner = lax.psum_scatter(inner, "tp", scatter_dimension=0, tiled=True)
    inner = lax.all_gather(inner, "rep", axis=1, tiled=True)
    gathered = lax.all_gather(half_out, ("rep", "tp"), axis=1, tiled=True)
    stacked = gathered.reshape(half_out.shape[0], reps, -1)
    full_out = jnp.transpose(stacked, (1, 0, 2)).reshape(half_out.shape[0] * reps, -1)
    full_out = lax.dynamic_slice_in_dim(full_out, lax.axis_index("rep") * width, width, 1)
    high, low = split_high_low(factor_scale * inner)
    spread = jnp.concatenate([high, low], axis=1)
    doubled = jnp.concatenate([full_out, full_out], axis=0)
    partial = jnp.dot(x, base, preferred_element_type=jnp.float32)
    summed = lax.psum_scatter(partial, "tp", scatter_dimension=0, tiled=True)
    decoded = summed + jnp.dot(spread, doubled, preferred_element_type=jnp.float32)
    return (decoded, new_in.T, new_out, first_in.T, second_in.T, first_out, second_out)


LINE = (((0, 1), (3, 2)), ((1, 2), (2, 1)), ((2, 3), (1, 0)))
(SEND_ROW, SECOND_AT, THIRD_AT, THIRD_FROM, OWN, FIRST_OWN, SECOND_OWN, ORDER, CORE_BIT, CHIP_BIT) = (
    0, 1, 2, 3, 4, 5, 6, 7, 11, 12)
MOST = 2048


def place_numbers(share):
    me, rep = lax.axis_index("tp"), lax.axis_index("rep")
    low = me < 2
    order = [me, me ^ 1, jnp.where(low, 2, 1), jnp.where(low, 3, 0)]
    numbers = [
        jnp.where(me == 0, share, 0),
        jnp.where(me == 1, 1, 0),
        jnp.where(me == 2, 3, 0),
        jnp.where(me == 2, 1, 0),
        me,
        jnp.where(me == 1, 0, 2),
        jnp.where(me == 2, 0, 1),
    ]
    numbers += [rank ^ rep for rank in order] + [rep & 1, rep >> 1]
    return jnp.stack([jnp.asarray(n, jnp.int32) for n in numbers])


def call(body, place, operands, specs, earlier, out_shapes, out_specs, grid=(1,), flops=0, moved=0):
    count = len(operands)

    def kernel(place_ref, *refs):
        body(place_ref, *refs[:count], *refs[count + len(earlier):])

    return pl.pallas_call(
        kernel,
        grid_spec=pltpu.PrefetchScalarGridSpec(
            num_scalar_prefetch=1,
            grid=grid,
            in_specs=list(specs) + [pl.BlockSpec(memory_space=pl.ANY)] * len(earlier),
            out_specs=out_specs,
        ),
        out_shape=out_shapes,
        compiler_params=pltpu.CompilerParams(vmem_limit_bytes=VMEM_BYTES),
        cost_estimate=pl.CostEstimate(flops=WEIGHT * flops, bytes_accessed=WEIGHT * moved, transcendentals=0),
    )(place, *operands, *earlier)


def whole(shape):
    return pl.BlockSpec(shape, lambda *_: (0,) * len(shape))


def block_width(start, width, most):
    block = min(most, width)
    while start % block or width % block:
        block //= 2
    return block


def matmul_chunk(place, x, base, start, width, share, earlier, most):
    rows, depth = x.shape
    block = block_width(start, width, most)
    sent = rows - share

    def body(place_ref, x_ref, base_ref, partial_ref, send_ref):
        partial_ref[...] = jnp.dot(x_ref[...], base_ref[...], preferred_element_type=jnp.float32)
        row = pl.multiple_of(place_ref[SEND_ROW], share)
        send_ref[...] = partial_ref[pl.ds(row, sent), :].astype(jnp.bfloat16)

    return call(
        body,
        place,
        [x, base],
        [whole(x.shape), pl.BlockSpec((depth, block), lambda j, p: (0, start // block + j))],
        earlier,
        [jax.ShapeDtypeStruct((rows, width), jnp.float32), jax.ShapeDtypeStruct((sent, width), jnp.bfloat16)],
        [pl.BlockSpec((rows, block), lambda j, p: (0, j)), pl.BlockSpec((sent, block), lambda j, p: (0, j))],
        grid=(width // block,),
        flops=2 * rows * depth * width,
        moved=2 * depth * width,
    )


def add_second(place, pieces, share, earlier):
    operands, specs = [], []
    for partial, arrived in pieces:
        width = partial.shape[1]
        operands += [partial, arrived, arrived]
        specs += [
            pl.BlockSpec((2 * share, width), lambda j, p: (p[SECOND_AT], 0)),
            pl.BlockSpec((share, width), lambda j, p: (p[SECOND_AT], 0)),
            pl.BlockSpec((share, width), lambda j, p: (p[SECOND_AT] + 1, 0)),
        ]
    widths = [partial.shape[1] for partial, _ in pieces]

    def body(place_ref, *refs):
        out_ref, at = refs[-1], 0
        for i, width in enumerate(widths):
            partial_ref, upper_ref, lower_ref = refs[3 * i:3 * i + 3]
            to = slice(at, at + width)
            out_ref[:share, to] = (partial_ref[:share, :] + upper_ref[...].astype(jnp.float32)).astype(jnp.bfloat16)
            out_ref[share:, to] = (partial_ref[share:, :] + lower_ref[...].astype(jnp.float32)).astype(jnp.bfloat16)
            at += width

    shape = (2 * share, sum(widths))
    return call(
        body, place, operands, specs, earlier, jax.ShapeDtypeStruct(shape, jnp.bfloat16), whole(shape),
        moved=16 * share * shape[1],
    )


def add_third(place, pieces, share, earlier):
    operands, specs = [], []
    for partial, arrived, _ in pieces:
        operands += [partial, arrived]
        specs += [
            pl.BlockSpec((share, partial.shape[1]), lambda j, p: (p[THIRD_AT], 0)),
            pl.BlockSpec((share, arrived.shape[1]), lambda j, p: (p[THIRD_FROM], 0)),
        ]
    widths = [partial.shape[1] for partial, _, _ in pieces]
    inside = [at for _, _, at in pieces]

    def body(place_ref, *refs):
        out_ref, at = refs[-1], 0
        for i, width in enumerate(widths):
            partial_ref, arrived_ref = refs[2 * i:2 * i + 2]
            arrived = arrived_ref[:, inside[i]:inside[i] + width].astype(jnp.float32)
            out_ref[:, at:at + width] = (partial_ref[...] + arrived).astype(jnp.bfloat16)
            at += width

    shape = (share, sum(widths))
    return call(
        body, place, operands, specs, earlier, jax.ShapeDtypeStruct(shape, jnp.bfloat16), whole(shape),
        moved=8 * share * shape[1],
    )


def finish_chunks(place, pieces, spread, factors, share, earlier, full_width=None, done=()):
    operands, specs = [spread], [whole(spread.shape)]
    half = factors[0].shape[0]
    for start, partial, first, second, _, third, _ in pieces:
        width = partial.shape[1]
        operands += [partial, first, second, third, *factors]
        specs += [
            pl.BlockSpec((share, width), lambda j, p: (p[OWN], 0)),
            pl.BlockSpec((share, width), lambda j, p: (p[FIRST_OWN], 0)),
            pl.BlockSpec((share, second.shape[1]), lambda j, p: (p[SECOND_OWN], 0)),
            whole(third.shape),
        ] + [pl.BlockSpec((half, width), lambda j, p, at=start // width: (0, at))] * 3
    for columns, _ in done:
        operands.append(columns)
        specs.append(whole(columns.shape))
    places = [(start, partial.shape[1], two, three) for start, partial, _, _, two, _, three in pieces]
    shape = (share, sum(width for _, width, _, _ in places) if full_width is None else full_width)

    def body(place_ref, spread_ref, *refs):
        out_ref, at = refs[-1], 0
        for i, (start, width, two, three) in enumerate(places):
            own_ref, first_ref, second_ref, third_ref, pair_ref, near_ref, far_ref = refs[7 * i:7 * i + 7]
            other = near_ref[...] + far_ref[...]
            ranks = jnp.concatenate([pair_ref[...], other, pair_ref[...], other], axis=0)
            total = own_ref[...] + first_ref[...].astype(jnp.float32)
            total = total + second_ref[:, two:two + width].astype(jnp.float32)
            total = total + third_ref[:, three:three + width].astype(jnp.float32)
            total = total + jnp.dot(spread_ref[...], ranks, preferred_element_type=jnp.float32)
            to = at if full_width is None else start
            out_ref[:, to:to + width] = total
            at += width
        for ref, (_, parts) in zip(refs[7 * len(places):], done):
            at = 0
            for start, width in parts:
                out_ref[:, start:start + width] = ref[:, at:at + width]
                at += width

    return call(
        body, place, operands, specs, earlier, jax.ShapeDtypeStruct(shape, jnp.float32), whole(shape),
        moved=14 * share * shape[1],
    )


def gradients_out(place, part_in, part_out, earlier):
    features, columns = part_in.shape[3], part_out.shape[3]
    rows = 2 * part_in.shape[2]

    def body(place_ref, in_ref, out_ref, send_ref):
        send_ref[:, :features] = in_ref[...].reshape(rows, features).astype(jnp.bfloat16)
        send_ref[:, features:] = out_ref[...].reshape(rows, columns).astype(jnp.bfloat16)

    shape = (rows, features + columns)
    return call(
        body,
        place,
        [part_in, part_out],
        [
            pl.BlockSpec((2, 1, rows // 2, n), lambda j, p: (0, 1 - p[CORE_BIT], 0, 0))
            for n in (features, columns)
        ],
        earlier,
        jax.ShapeDtypeStruct(shape, jnp.bfloat16),
        whole(shape),
        moved=6 * shape[0] * shape[1],
    )


def gradients_on(place, part_in, part_out, arrived, earlier):
    features, columns = part_in.shape[3], part_out.shape[3]
    ranks = part_in.shape[2]

    def body(place_ref, in_ref, out_ref, arrived_ref, send_ref, keep_ref):
        upper = place_ref[CHIP_BIT] == 0
        for ref, at, n in ((in_ref, 0, features), (out_ref, features, columns)):
            total = ref[...].reshape(2 * ranks, n) + arrived_ref[:, at:at + n].astype(jnp.float32)
            keep_ref[:, at:at + n] = jnp.where(upper, total[:ranks], total[ranks:])
            send_ref[:, at:at + n] = jnp.where(upper, total[ranks:], total[:ranks]).astype(jnp.bfloat16)

    shape = (ranks, features + columns)
    return call(
        body,
        place,
        [part_in, part_out, arrived],
        [pl.BlockSpec((2, 1, ranks, n), lambda j, p: (0, p[CORE_BIT], 0, 0)) for n in (features, columns)]
        + [whole(arrived.shape)],
        earlier,
        [jax.ShapeDtypeStruct(shape, jnp.bfloat16), jax.ShapeDtypeStruct(shape, jnp.float32)],
        [whole(shape)] * 2,
        moved=20 * shape[0] * shape[1],
    )


def update_factors(place, keep, arrived, in_state, out_state, earlier):
    features, columns = in_state[0].shape[1], out_state[0].shape[1]
    ranks = keep.shape[0]

    def body(place_ref, keep_ref, arrived_ref, *refs):
        for side, at, n in ((0, 0, features), (1, features, columns)):
            weights, first, second = refs[3 * side:3 * side + 3]
            outs = refs[6 + 4 * side:10 + 4 * side]
            grads = keep_ref[:, at:at + n] + arrived_ref[:, at:at + n].astype(jnp.float32)
            values = apply_adam_rule(weights[...], first[...], second[...], grads)
            for out, value in zip(outs, values):
                out[...] = value
            outs[3][...] = values[0].astype(jnp.bfloat16)

    operands = [keep, arrived, *in_state, *out_state]
    shapes = []
    for n in (features, columns):
        shapes += [jax.ShapeDtypeStruct((ranks, n), jnp.float32)] * 3 + [jax.ShapeDtypeStruct((ranks, n), jnp.bfloat16)]
    return call(
        body,
        place,
        operands,
        [whole(o.shape) for o in operands],
        earlier,
        shapes,
        [whole(s.shape) for s in shapes],
        moved=32 * ranks * (features + columns),
    )


def inner_products(place, x, near, far, turned, earlier):
    rows, ranks = x.shape[0], turned.shape[0]
    width = turned.shape[1]
    inner_width = 4 * rows

    def body(place_ref, x_ref, near_ref, far_ref, turned_ref, inner_ref, send_ref):
        for i, ref in enumerate((near_ref, far_ref)):
            products = lax.dot_general(
                ref[...], x_ref[...], (((1,), (1,)), ((), ())), preferred_element_type=jnp.float32
            )
            for j in range(2):
                at = (2 * i + j) * rows
                inner_ref[:, at:at + rows] = products[j * ranks:(j + 1) * ranks]
        high, low = split_high_low(inner_ref[...])
        send_ref[:, :width] = turned_ref[...]
        send_ref[:, width:width + inner_width] = high
        send_ref[:, width + inner_width:] = low

    shapes = [(ranks, inner_width), (ranks, width + 2 * inner_width)]
    return call(
        body,
        place,
        [x, near, far, turned],
        [whole(x.shape), whole(near.shape), whole(far.shape), whole(turned.shape)],
        earlier,
        [jax.ShapeDtypeStruct(shapes[0], jnp.float32), jax.ShapeDtypeStruct(shapes[1], jnp.bfloat16)],
        [whole(shape) for shape in shapes],
        flops=8 * rows * ranks * x.shape[1],
        moved=2 * rows * x.shape[1],
    )


def join_pair(place, turned, swapped, inner, earlier):
    ranks, width = turned.shape
    inner_width = inner.shape[1]

    def body(place_ref, turned_ref, swapped_ref, inner_ref, pair_ref, sum_ref):
        both = [turned_ref[...].astype(jnp.float32), swapped_ref[:, :width].astype(jnp.float32)]
        pair_ref[:, :width] = jnp.concatenate(both, axis=0).astype(jnp.bfloat16)
        total = inner_ref[...] + swapped_ref[:, width:width + inner_width].astype(jnp.float32)
        total = total + swapped_ref[:, width + inner_width:].astype(jnp.float32)
        sum_ref[...] = total
        halves = [half.astype(jnp.float32) for half in split_high_low(total)]
        pair_ref[:, width:] = jnp.concatenate(halves, axis=0).astype(jnp.bfloat16)

    shapes = [(2 * ranks, width + inner_width), (ranks, inner_width)]
    return call(
        body,
        place,
        [turned, swapped, inner],
        [whole(turned.shape), whole(swapped.shape), whole(inner.shape)],
        earlier,
        [jax.ShapeDtypeStruct(shapes[0], jnp.bfloat16), jax.ShapeDtypeStruct(shapes[1], jnp.float32)],
        [whole(shape) for shape in shapes],
        moved=8 * ranks * width,
    )


def spread_inner(place, inner, near, far, width, share, earlier):
    portion = inner.shape[0]
    rows = inner.shape[1] // 4
    ranks = 4 * portion

    def body(place_ref, inner_ref, near_ref, far_ref, out_ref):
        other = near_ref[:, width:].astype(jnp.float32) + far_ref[:, width:].astype(jnp.float32)
        total = factor_scale * (inner_ref[...] + (other[:portion] + other[portion:]))
        total = jnp.concatenate([total[:, i * rows:(i + 1) * rows] for i in range(4)], axis=0)
        shape = (share, rows)
        mine = lax.broadcasted_iota(jnp.int32, shape, 0) + place_ref[OWN] * share
        mine = jnp.where(lax.broadcasted_iota(jnp.int32, shape, 1) == mine, 1.0, 0.0).astype(jnp.bfloat16)
        block = lax.broadcasted_iota(jnp.int32, (ranks, ranks), 1) // portion
        source = jnp.full((ranks, ranks), 0, jnp.int32)
        for i in range(4):
            source = jnp.where(block == i, place_ref[ORDER + i], source)
        column = lax.broadcasted_iota(jnp.int32, (ranks, ranks), 1) % portion
        chosen = lax.broadcasted_iota(jnp.int32, (ranks, ranks), 0) == source * portion + column
        chosen = jnp.where(chosen, 1.0, 0.0).astype(jnp.bfloat16)
        halves = []
        for half in split_high_low(total):
            turned = lax.dot_general(mine, half, (((1,), (1,)), ((), ())), preferred_element_type=jnp.float32)
            halves.append(jnp.dot(turned.astype(jnp.bfloat16), chosen, preferred_element_type=jnp.float32))
        out_ref[...] = jnp.concatenate(halves, axis=1).astype(jnp.bfloat16)

    return call(
        body,
        place,
        [inner, near, far],
        [whole(inner.shape), whole(near.shape), whole(far.shape)],
        earlier,
        jax.ShapeDtypeStruct((share, 2 * ranks), jnp.bfloat16),
        whole((share, 2 * ranks)),
    )


def local_line(
    base,
    decoded_row_activations,
    input_factor,
    output_factor,
    input_first_moment,
    input_second_moment,
    output_first_moment,
    output_second_moment,
    replica_input_gradient,
    replica_output_gradient,
):
    x = decoded_row_activations
    width = base.shape[1]
    share = x.shape[0] // 4
    ranks = input_factor.shape[1]
    place = place_numbers(share)
    part_in = replica_input_gradient[0].T.reshape(2, 2, ranks, -1)
    part_out = replica_output_gradient[0].reshape(2, 2, ranks, -1)

    unit = width // 20
    starts = [unit * at for at, _ in CHUNKS]
    widths = [unit * wide for _, wide in CHUNKS]
    partials, firsts, seconds, thirds = {}, {}, {}, {}

    def line(step, values):
        return lax.ppermute(values, "tp", LINE[step])

    def chip(bit, values):
        return lax.ppermute(values, "rep", [(i, i ^ bit) for i in range(4)])

    def matmul(c, *earlier):
        partials[c], send = matmul_chunk(place, x, base, starts[c], widths[c], share, earlier, 512)
        firsts[c] = line(0, send)
        return send

    def second(chunks, *earlier):
        send = add_second(place, [(partials[c], firsts[c]) for c in chunks], share, earlier)
        got, at = line(1, send), 0
        for c in chunks:
            seconds[c] = (got, at)
            at += widths[c]
        return send

    def third(chunks, *earlier):
        send = add_third(place, [(partials[c], *seconds[c]) for c in chunks], share, earlier)
        got, at = line(2, send), 0
        for c in chunks:
            thirds[c] = (got, at)
            at += widths[c]
        return send

    def finish(chunks, *earlier, full_width=None, done=()):
        pieces = [(starts[c], partials[c], firsts[c], *seconds[c], *thirds[c]) for c in chunks]
        columns = finish_chunks(place, pieces, spread, factors, share, earlier, full_width, done)
        finished.append((columns, [(starts[c], widths[c]) for c in chunks]))
        return columns

    finished = []
    last = matmul(0)
    last = gradients_out(place, part_in, part_out, [last])
    from_core = chip(1, last)
    last = matmul(1, last)
    across, keep = gradients_on(place, part_in, part_out, from_core, [last])
    from_chip = chip(2, across)
    last = matmul(2, keep)
    in_state = (input_factor.T, input_first_moment.T, input_second_moment.T)
    out_state = (output_factor, output_first_moment, output_second_moment)
    states = update_factors(place, keep, from_chip, in_state, out_state, [last])
    new_in, first_in, second_in, half_in, new_out, first_out, second_out, half_out = states
    turned = lax.ppermute(half_out, ("rep", "tp"), [(4 * a + b, 4 * b + a) for a in range(4) for b in range(4)])
    near_in = jnp.concatenate([half_in, chip(1, half_in)], axis=0)
    far_in = chip(2, near_in)
    last = second((0, 1), half_out)
    last = matmul(3, last)
    inner, last = inner_products(place, x, near_in, far_in, turned, [last])
    swapped = lax.ppermute(last, "tp", [(i, i ^ 1) for i in range(4)])
    last = second((2,), last)
    last = matmul(4, last)
    last = second((3,), last)
    last = third((0, 1, 2), last)
    pair, inner = join_pair(place, turned, swapped, inner, [last])
    near_out = line(1, pair)
    last = matmul(5, pair)
    last = matmul(6, last)
    last = second((4,), last, thirds[0][0])
    far_out = line(2, near_out)
    factors = (pair, near_out, far_out)
    last = second((5,), last)
    last = third((3,), last)
    last = second((6,), last)
    last = spread = spread_inner(place, inner, near_out, far_out, width, share, [last])
    last = finish((0, 1, 2), last)
    last = third((4,), last)
    last = third((5,), last)
    last = third((6,), last)
    last = finish((3,), last)
    last = finish((4,), last)
    decoded = finish((5, 6), last, full_width=width, done=list(finished))
    return (decoded, new_in.T, new_out, first_in.T, second_in.T, first_out, second_out)


def solution(mesh):
    line = mesh.shape["rep"] == 4 and mesh.shape["tp"] == 4
    return jax.shard_map(
        local_line if line else local_any,
        mesh=mesh,
        in_specs=(
            P("tp", "rep"),
            P("groups", "tp"),
            P(("groups", "tp"), "rep"),
            P("rep", ("groups", "tp")),
            P(("groups", "tp"), "rep"),
            P(("groups", "tp"), "rep"),
            P("rep", ("groups", "tp")),
            P("rep", ("groups", "tp")),
            P("rep", ("groups", "tp"), None),
            P("rep", None, ("groups", "tp")),
        ),
        out_specs=(
            P(("groups", "tp"), "rep"),
            P(("groups", "tp"), "rep"),
            P("rep", ("groups", "tp")),
            P(("groups", "tp"), "rep"),
            P(("groups", "tp"), "rep"),
            P("rep", ("groups", "tp")),
            P("rep", ("groups", "tp")),
        ),
        check_vma=False,
    )
```

```python
import jax
import jax.numpy as jnp
from jax import lax
from jax.experimental import pallas as pl
from jax.experimental.pallas import tpu as pltpu
from jax.sharding import PartitionSpec as P

ADAM_STEP = 200


beta_one = 0.9
beta_two = 0.999
learn_rate = 0.003
adam_eps = 1e-08
factor_scale = 2.0

CHUNKS = ((16, 2), (12, 3), (0, 4), (4, 4), (8, 4), (18, 2), (15, 1))
VMEM_BYTES = 40 * 1024 * 1024
WEIGHT = 5


def apply_adam_rule(weights, moment, second, grads):
    moment_new = beta_one * moment + (1.0 - beta_one) * grads
    second_new = beta_two * second + (1.0 - beta_two) * grads * grads
    first_fix = 1.0 - beta_one**ADAM_STEP
    second_fix = 1.0 - beta_two**ADAM_STEP
    step_size = moment_new / first_fix / (jnp.sqrt(second_new / second_fix) + adam_eps)
    return (weights - learn_rate * step_size, moment_new, second_new)


def scatter_sum_rep(part):
    reps = lax.axis_size("rep")
    me = lax.axis_index("rep")
    share = part.shape[0] // reps
    blocks = part.reshape(reps, share, part.shape[1])
    bit = 1
    while bit < reps:
        pairs = blocks.reshape(blocks.shape[0] // 2, 2, share, part.shape[1])
        mine_bit = (me // bit) % 2
        keep = lax.dynamic_index_in_dim(pairs, mine_bit, 1, keepdims=False)
        send = lax.dynamic_index_in_dim(pairs, 1 - mine_bit, 1, keepdims=False)
        got = lax.ppermute(send.astype(jnp.bfloat16), "rep", [(i, i ^ bit) for i in range(reps)])
        blocks = keep + got.astype(jnp.float32)
        bit *= 2
    return blocks[0]


def split_high_low(values):
    high = values.astype(jnp.bfloat16)
    low = (values - high.astype(jnp.float32)).astype(jnp.bfloat16)
    return high, low


def local_any(
    base,
    decoded_row_activations,
    input_factor,
    output_factor,
    input_first_moment,
    input_second_moment,
    output_first_moment,
    output_second_moment,
    replica_input_gradient,
    replica_output_gradient,
):
    x = decoded_row_activations
    width = base.shape[1]
    features = base.shape[0]
    reps = lax.axis_size("rep")
    part = jnp.concatenate([replica_input_gradient[0].T, replica_output_gradient[0]], axis=1)
    grads = scatter_sum_rep(part)
    grads_in, grads_out = grads[:, :features], grads[:, features:]
    new_in, first_in, second_in = apply_adam_rule(input_factor.T, input_first_moment.T, input_second_moment.T, grads_in)
    new_out, first_out, second_out = apply_adam_rule(output_factor, output_first_moment, output_second_moment, grads_out)
    half_in = new_in.astype(jnp.bfloat16)
    half_out = new_out.astype(jnp.bfloat16)
    inner = lax.dot_general(x, half_in, (((1,), (1,)), ((), ())), preferred_element_type=jnp.float32)
    inner = lax.psum_scatter(inner, "tp", scatter_dimension=0, tiled=True)
    inner = lax.all_gather(inner, "rep", axis=1, tiled=True)
    gathered = lax.all_gather(half_out, ("rep", "tp"), axis=1, tiled=True)
    stacked = gathered.reshape(half_out.shape[0], reps, -1)
    full_out = jnp.transpose(stacked, (1, 0, 2)).reshape(half_out.shape[0] * reps, -1)
    full_out = lax.dynamic_slice_in_dim(full_out, lax.axis_index("rep") * width, width, 1)
    high, low = split_high_low(factor_scale * inner)
    spread = jnp.concatenate([high, low], axis=1)
    doubled = jnp.concatenate([full_out, full_out], axis=0)
    partial = jnp.dot(x, base, preferred_element_type=jnp.float32)
    summed = lax.psum_scatter(partial, "tp", scatter_dimension=0, tiled=True)
    decoded = summed + jnp.dot(spread, doubled, preferred_element_type=jnp.float32)
    return (decoded, new_in.T, new_out, first_in.T, second_in.T, first_out, second_out)


LINE = (((0, 1), (3, 2)), ((1, 2), (2, 1)), ((2, 3), (1, 0)))
(SEND_ROW, SECOND_AT, THIRD_AT, THIRD_FROM, OWN, FIRST_OWN, SECOND_OWN, ORDER, CORE_BIT, CHIP_BIT) = (
    0, 1, 2, 3, 4, 5, 6, 7, 11, 12)
MOST = 2048


def place_numbers(share):
    me, rep = lax.axis_index("tp"), lax.axis_index("rep")
    low = me < 2
    order = [me, me ^ 1, jnp.where(low, 2, 1), jnp.where(low, 3, 0)]
    numbers = [
        jnp.where(me == 0, share, 0),
        jnp.where(me == 1, 1, 0),
        jnp.where(me == 2, 3, 0),
        jnp.where(me == 2, 1, 0),
        me,
        jnp.where(me == 1, 0, 2),
        jnp.where(me == 2, 0, 1),
    ]
    numbers += [rank ^ rep for rank in order] + [rep & 1, rep >> 1]
    return jnp.stack([jnp.asarray(n, jnp.int32) for n in numbers])


def call(body, place, operands, specs, earlier, out_shapes, out_specs, grid=(1,), flops=0, moved=0):
    count = len(operands)

    def kernel(place_ref, *refs):
        body(place_ref, *refs[:count], *refs[count + len(earlier):])

    return pl.pallas_call(
        kernel,
        grid_spec=pltpu.PrefetchScalarGridSpec(
            num_scalar_prefetch=1,
            grid=grid,
            in_specs=list(specs) + [pl.BlockSpec(memory_space=pl.ANY)] * len(earlier),
            out_specs=out_specs,
        ),
        out_shape=out_shapes,
        compiler_params=pltpu.CompilerParams(vmem_limit_bytes=VMEM_BYTES),
        cost_estimate=pl.CostEstimate(flops=WEIGHT * flops, bytes_accessed=WEIGHT * moved, transcendentals=0),
    )(place, *operands, *earlier)


def whole(shape):
    return pl.BlockSpec(shape, lambda *_: (0,) * len(shape))


def block_width(start, width, most):
    block = min(most, width)
    while start % block or width % block:
        block //= 2
    return block


def matmul_chunk(place, x, base, start, width, share, earlier, most):
    rows, depth = x.shape
    block = block_width(start, width, most)
    sent = rows - share

    def body(place_ref, x_ref, base_ref, partial_ref, send_ref):
        partial_ref[...] = jnp.dot(x_ref[...], base_ref[...], preferred_element_type=jnp.float32)
        row = pl.multiple_of(place_ref[SEND_ROW], share)
        send_ref[...] = partial_ref[pl.ds(row, sent), :].astype(jnp.bfloat16)

    return call(
        body,
        place,
        [x, base],
        [whole(x.shape), pl.BlockSpec((depth, block), lambda j, p: (0, start // block + j))],
        earlier,
        [jax.ShapeDtypeStruct((rows, width), jnp.float32), jax.ShapeDtypeStruct((sent, width), jnp.bfloat16)],
        [pl.BlockSpec((rows, block), lambda j, p: (0, j)), pl.BlockSpec((sent, block), lambda j, p: (0, j))],
        grid=(width // block,),
        flops=2 * rows * depth * width,
        moved=2 * depth * width,
    )


def add_second(place, pieces, share, earlier):
    operands, specs = [], []
    for partial, arrived in pieces:
        width = partial.shape[1]
        operands += [partial, arrived, arrived]
        specs += [
            pl.BlockSpec((2 * share, width), lambda j, p: (p[SECOND_AT], 0)),
            pl.BlockSpec((share, width), lambda j, p: (p[SECOND_AT], 0)),
            pl.BlockSpec((share, width), lambda j, p: (p[SECOND_AT] + 1, 0)),
        ]
    widths = [partial.shape[1] for partial, _ in pieces]

    def body(place_ref, *refs):
        out_ref, at = refs[-1], 0
        for i, width in enumerate(widths):
            partial_ref, upper_ref, lower_ref = refs[3 * i:3 * i + 3]
            to = slice(at, at + width)
            out_ref[:share, to] = (partial_ref[:share, :] + upper_ref[...].astype(jnp.float32)).astype(jnp.bfloat16)
            out_ref[share:, to] = (partial_ref[share:, :] + lower_ref[...].astype(jnp.float32)).astype(jnp.bfloat16)
            at += width

    shape = (2 * share, sum(widths))
    return call(
        body, place, operands, specs, earlier, jax.ShapeDtypeStruct(shape, jnp.bfloat16), whole(shape),
        moved=16 * share * shape[1],
    )


def add_third(place, pieces, share, earlier):
    operands, specs = [], []
    for partial, arrived, _ in pieces:
        operands += [partial, arrived]
        specs += [
            pl.BlockSpec((share, partial.shape[1]), lambda j, p: (p[THIRD_AT], 0)),
            pl.BlockSpec((share, arrived.shape[1]), lambda j, p: (p[THIRD_FROM], 0)),
        ]
    widths = [partial.shape[1] for partial, _, _ in pieces]
    inside = [at for _, _, at in pieces]

    def body(place_ref, *refs):
        out_ref, at = refs[-1], 0
        for i, width in enumerate(widths):
            partial_ref, arrived_ref = refs[2 * i:2 * i + 2]
            arrived = arrived_ref[:, inside[i]:inside[i] + width].astype(jnp.float32)
            out_ref[:, at:at + width] = (partial_ref[...] + arrived).astype(jnp.bfloat16)
            at += width

    shape = (share, sum(widths))
    return call(
        body, place, operands, specs, earlier, jax.ShapeDtypeStruct(shape, jnp.bfloat16), whole(shape),
        moved=8 * share * shape[1],
    )


def finish_chunks(place, pieces, spread, factors, share, earlier, full_width=None, done=()):
    operands, specs = [spread], [whole(spread.shape)]
    half = factors[0].shape[0]
    for start, partial, first, second, _, third, _ in pieces:
        width = partial.shape[1]
        operands += [partial, first, second, third, *factors]
        specs += [
            pl.BlockSpec((share, width), lambda j, p: (p[OWN], 0)),
            pl.BlockSpec((share, width), lambda j, p: (p[FIRST_OWN], 0)),
            pl.BlockSpec((share, second.shape[1]), lambda j, p: (p[SECOND_OWN], 0)),
            whole(third.shape),
        ] + [pl.BlockSpec((half, width), lambda j, p, at=start // width: (0, at))] * 3
    for columns, _ in done:
        operands.append(columns)
        specs.append(whole(columns.shape))
    places = [(start, partial.shape[1], two, three) for start, partial, _, _, two, _, three in pieces]
    shape = (share, sum(width for _, width, _, _ in places) if full_width is None else full_width)

    def body(place_ref, spread_ref, *refs):
        out_ref, at = refs[-1], 0
        for i, (start, width, two, three) in enumerate(places):
            own_ref, first_ref, second_ref, third_ref, pair_ref, near_ref, far_ref = refs[7 * i:7 * i + 7]
            other = near_ref[...] + far_ref[...]
            ranks = jnp.concatenate([pair_ref[...], other, pair_ref[...], other], axis=0)
            total = own_ref[...] + first_ref[...].astype(jnp.float32)
            total = total + second_ref[:, two:two + width].astype(jnp.float32)
            total = total + third_ref[:, three:three + width].astype(jnp.float32)
            total = total + jnp.dot(spread_ref[...], ranks, preferred_element_type=jnp.float32)
            to = at if full_width is None else start
            out_ref[:, to:to + width] = total
            at += width
        for ref, (_, parts) in zip(refs[7 * len(places):], done):
            at = 0
            for start, width in parts:
                out_ref[:, start:start + width] = ref[:, at:at + width]
                at += width

    return call(
        body, place, operands, specs, earlier, jax.ShapeDtypeStruct(shape, jnp.float32), whole(shape),
        moved=14 * share * shape[1],
    )


def gradients_out(place, part_in, part_out, earlier):
    features, columns = part_in.shape[3], part_out.shape[3]
    rows = 2 * part_in.shape[2]

    def body(place_ref, in_ref, out_ref, send_ref):
        send_ref[:, :features] = in_ref[...].reshape(rows, features).astype(jnp.bfloat16)
        send_ref[:, features:] = out_ref[...].reshape(rows, columns).astype(jnp.bfloat16)

    shape = (rows, features + columns)
    return call(
        body,
        place,
        [part_in, part_out],
        [
            pl.BlockSpec((2, 1, rows // 2, n), lambda j, p: (0, 1 - p[CORE_BIT], 0, 0))
            for n in (features, columns)
        ],
        earlier,
        jax.ShapeDtypeStruct(shape, jnp.bfloat16),
        whole(shape),
        moved=6 * shape[0] * shape[1],
    )


def gradients_on(place, part_in, part_out, arrived, earlier):
    features, columns = part_in.shape[3], part_out.shape[3]
    ranks = part_in.shape[2]

    def body(place_ref, in_ref, out_ref, arrived_ref, send_ref, keep_ref):
        upper = place_ref[CHIP_BIT] == 0
        for ref, at, n in ((in_ref, 0, features), (out_ref, features, columns)):
            total = ref[...].reshape(2 * ranks, n) + arrived_ref[:, at:at + n].astype(jnp.float32)
            keep_ref[:, at:at + n] = jnp.where(upper, total[:ranks], total[ranks:])
            send_ref[:, at:at + n] = jnp.where(upper, total[ranks:], total[:ranks]).astype(jnp.bfloat16)

    shape = (ranks, features + columns)
    return call(
        body,
        place,
        [part_in, part_out, arrived],
        [pl.BlockSpec((2, 1, ranks, n), lambda j, p: (0, p[CORE_BIT], 0, 0)) for n in (features, columns)]
        + [whole(arrived.shape)],
        earlier,
        [jax.ShapeDtypeStruct(shape, jnp.bfloat16), jax.ShapeDtypeStruct(shape, jnp.float32)],
        [whole(shape)] * 2,
        moved=20 * shape[0] * shape[1],
    )


def update_factors(place, keep, arrived, in_state, out_state, earlier):
    features, columns = in_state[0].shape[1], out_state[0].shape[1]
    ranks = keep.shape[0]

    def body(place_ref, keep_ref, arrived_ref, *refs):
        for side, at, n in ((0, 0, features), (1, features, columns)):
            weights, first, second = refs[3 * side:3 * side + 3]
            outs = refs[6 + 4 * side:10 + 4 * side]
            grads = keep_ref[:, at:at + n] + arrived_ref[:, at:at + n].astype(jnp.float32)
            values = apply_adam_rule(weights[...], first[...], second[...], grads)
            for out, value in zip(outs, values):
                out[...] = value
            outs[3][...] = values[0].astype(jnp.bfloat16)

    operands = [keep, arrived, *in_state, *out_state]
    shapes = []
    for n in (features, columns):
        shapes += [jax.ShapeDtypeStruct((ranks, n), jnp.float32)] * 3 + [jax.ShapeDtypeStruct((ranks, n), jnp.bfloat16)]
    return call(
        body,
        place,
        operands,
        [whole(o.shape) for o in operands],
        earlier,
        shapes,
        [whole(s.shape) for s in shapes],
        moved=32 * ranks * (features + columns),
    )


def inner_products(place, x, near, far, turned, earlier):
    rows, ranks = x.shape[0], turned.shape[0]
    width = turned.shape[1]
    inner_width = 4 * rows

    def body(place_ref, x_ref, near_ref, far_ref, turned_ref, inner_ref, send_ref):
        for i, ref in enumerate((near_ref, far_ref)):
            products = lax.dot_general(
                ref[...], x_ref[...], (((1,), (1,)), ((), ())), preferred_element_type=jnp.float32
            )
            for j in range(2):
                at = (2 * i + j) * rows
                inner_ref[:, at:at + rows] = products[j * ranks:(j + 1) * ranks]
        high, low = split_high_low(inner_ref[...])
        send_ref[:, :width] = turned_ref[...]
        send_ref[:, width:width + inner_width] = high
        send_ref[:, width + inner_width:] = low

    shapes = [(ranks, inner_width), (ranks, width + 2 * inner_width)]
    return call(
        body,
        place,
        [x, near, far, turned],
        [whole(x.shape), whole(near.shape), whole(far.shape), whole(turned.shape)],
        earlier,
        [jax.ShapeDtypeStruct(shapes[0], jnp.float32), jax.ShapeDtypeStruct(shapes[1], jnp.bfloat16)],
        [whole(shape) for shape in shapes],
        flops=8 * rows * ranks * x.shape[1],
        moved=2 * rows * x.shape[1],
    )


def join_pair(place, turned, swapped, inner, earlier):
    ranks, width = turned.shape
    inner_width = inner.shape[1]

    def body(place_ref, turned_ref, swapped_ref, inner_ref, pair_ref, sum_ref):
        both = [turned_ref[...].astype(jnp.float32), swapped_ref[:, :width].astype(jnp.float32)]
        pair_ref[:, :width] = jnp.concatenate(both, axis=0).astype(jnp.bfloat16)
        total = inner_ref[...] + swapped_ref[:, width:width + inner_width].astype(jnp.float32)
        total = total + swapped_ref[:, width + inner_width:].astype(jnp.float32)
        sum_ref[...] = total
        halves = [half.astype(jnp.float32) for half in split_high_low(total)]
        pair_ref[:, width:] = jnp.concatenate(halves, axis=0).astype(jnp.bfloat16)

    shapes = [(2 * ranks, width + inner_width), (ranks, inner_width)]
    return call(
        body,
        place,
        [turned, swapped, inner],
        [whole(turned.shape), whole(swapped.shape), whole(inner.shape)],
        earlier,
        [jax.ShapeDtypeStruct(shapes[0], jnp.bfloat16), jax.ShapeDtypeStruct(shapes[1], jnp.float32)],
        [whole(shape) for shape in shapes],
        moved=8 * ranks * width,
    )


def spread_inner(place, inner, near, far, width, share, earlier):
    portion = inner.shape[0]
    rows = inner.shape[1] // 4
    ranks = 4 * portion

    def body(place_ref, inner_ref, near_ref, far_ref, out_ref):
        other = near_ref[:, width:].astype(jnp.float32) + far_ref[:, width:].astype(jnp.float32)
        total = factor_scale * (inner_ref[...] + (other[:portion] + other[portion:]))
        total = jnp.concatenate([total[:, i * rows:(i + 1) * rows] for i in range(4)], axis=0)
        shape = (share, rows)
        mine = lax.broadcasted_iota(jnp.int32, shape, 0) + place_ref[OWN] * share
        mine = jnp.where(lax.broadcasted_iota(jnp.int32, shape, 1) == mine, 1.0, 0.0).astype(jnp.bfloat16)
        block = lax.broadcasted_iota(jnp.int32, (ranks, ranks), 1) // portion
        source = jnp.full((ranks, ranks), 0, jnp.int32)
        for i in range(4):
            source = jnp.where(block == i, place_ref[ORDER + i], source)
        column = lax.broadcasted_iota(jnp.int32, (ranks, ranks), 1) % portion
        chosen = lax.broadcasted_iota(jnp.int32, (ranks, ranks), 0) == source * portion + column
        chosen = jnp.where(chosen, 1.0, 0.0).astype(jnp.bfloat16)
        halves = []
        for half in split_high_low(total):
            turned = lax.dot_general(mine, half, (((1,), (1,)), ((), ())), preferred_element_type=jnp.float32)
            halves.append(jnp.dot(turned.astype(jnp.bfloat16), chosen, preferred_element_type=jnp.float32))
        out_ref[...] = jnp.concatenate(halves, axis=1).astype(jnp.bfloat16)

    return call(
        body,
        place,
        [inner, near, far],
        [whole(inner.shape), whole(near.shape), whole(far.shape)],
        earlier,
        jax.ShapeDtypeStruct((share, 2 * ranks), jnp.bfloat16),
        whole((share, 2 * ranks)),
    )


def local_line(
    base,
    decoded_row_activations,
    input_factor,
    output_factor,
    input_first_moment,
    input_second_moment,
    output_first_moment,
    output_second_moment,
    replica_input_gradient,
    replica_output_gradient,
):
    x = decoded_row_activations
    width = base.shape[1]
    share = x.shape[0] // 4
    ranks = input_factor.shape[1]
    place = place_numbers(share)
    part_in = replica_input_gradient[0].T.reshape(2, 2, ranks, -1)
    part_out = replica_output_gradient[0].reshape(2, 2, ranks, -1)

    unit = width // 20
    starts = [unit * at for at, _ in CHUNKS]
    widths = [unit * wide for _, wide in CHUNKS]
    partials, firsts, seconds, thirds = {}, {}, {}, {}

    def line(step, values):
        return lax.ppermute(values, "tp", LINE[step])

    def chip(bit, values):
        return lax.ppermute(values, "rep", [(i, i ^ bit) for i in range(4)])

    def matmul(c, *earlier):
        partials[c], send = matmul_chunk(place, x, base, starts[c], widths[c], share, earlier, 512)
        firsts[c] = line(0, send)
        return send

    def second(chunks, *earlier):
        send = add_second(place, [(partials[c], firsts[c]) for c in chunks], share, earlier)
        got, at = line(1, send), 0
        for c in chunks:
            seconds[c] = (got, at)
            at += widths[c]
        return send

    def third(chunks, *earlier):
        send = add_third(place, [(partials[c], *seconds[c]) for c in chunks], share, earlier)
        got, at = line(2, send), 0
        for c in chunks:
            thirds[c] = (got, at)
            at += widths[c]
        return send

    def finish(chunks, *earlier, full_width=None, done=()):
        pieces = [(starts[c], partials[c], firsts[c], *seconds[c], *thirds[c]) for c in chunks]
        columns = finish_chunks(place, pieces, spread, factors, share, earlier, full_width, done)
        finished.append((columns, [(starts[c], widths[c]) for c in chunks]))
        return columns

    finished = []
    last = matmul(0)
    last = gradients_out(place, part_in, part_out, [last])
    from_core = chip(1, last)
    last = matmul(1, last)
    across, keep = gradients_on(place, part_in, part_out, from_core, [last])
    from_chip = chip(2, across)
    last = matmul(2, keep)
    in_state = (input_factor.T, input_first_moment.T, input_second_moment.T)
    out_state = (output_factor, output_first_moment, output_second_moment)
    states = update_factors(place, keep, from_chip, in_state, out_state, [last])
    new_in, first_in, second_in, half_in, new_out, first_out, second_out, half_out = states
    turned = lax.ppermute(half_out, ("rep", "tp"), [(4 * a + b, 4 * b + a) for a in range(4) for b in range(4)])
    near_in = jnp.concatenate([half_in, chip(1, half_in)], axis=0)
    far_in = chip(2, near_in)
    last = second((0, 1), half_out)
    last = matmul(3, last)
    inner, last = inner_products(place, x, near_in, far_in, turned, [last])
    swapped = lax.ppermute(last, "tp", [(i, i ^ 1) for i in range(4)])
    last = second((2,), last)
    last = matmul(4, last)
    last = second((3,), last)
    last = third((0, 1, 2), last)
    pair, inner = join_pair(place, turned, swapped, inner, [last])
    near_out = line(1, pair)
    last = matmul(5, pair)
    last = third((3,), last)
    last = second((4,), last, thirds[0][0])
    last = matmul(6, last)
    far_out = line(2, near_out)
    factors = (pair, near_out, far_out)
    last = second((5,), last, thirds[3][0])
    last = second((6,), last)
    last = third((4,), last)
    last = third((5, 6), last)
    last = spread = spread_inner(place, inner, near_out, far_out, width, share, [last])
    last = finish((0, 1, 2), last)
    last = finish((3,), last)
    last = finish((4,), last)
    decoded = finish((5, 6), last, full_width=width, done=list(finished))
    return (decoded, new_in.T, new_out, first_in.T, second_in.T, first_out, second_out)


def solution(mesh):
    line = mesh.shape["rep"] == 4 and mesh.shape["tp"] == 4
    return jax.shard_map(
        local_line if line else local_any,
        mesh=mesh,
        in_specs=(
            P("tp", "rep"),
            P("groups", "tp"),
            P(("groups", "tp"), "rep"),
            P("rep", ("groups", "tp")),
            P(("groups", "tp"), "rep"),
            P(("groups", "tp"), "rep"),
            P("rep", ("groups", "tp")),
            P("rep", ("groups", "tp")),
            P("rep", ("groups", "tp"), None),
            P("rep", None, ("groups", "tp")),
        ),
        out_specs=(
            P(("groups", "tp"), "rep"),
            P(("groups", "tp"), "rep"),
            P("rep", ("groups", "tp")),
            P(("groups", "tp"), "rep"),
            P(("groups", "tp"), "rep"),
            P("rep", ("groups", "tp")),
            P("rep", ("groups", "tp")),
        ),
        check_vma=False,
    )
```

```python
import jax
import jax.numpy as jnp
from jax import lax
from jax.experimental import pallas as pl
from jax.experimental.pallas import tpu as pltpu
from jax.sharding import PartitionSpec as P

ADAM_STEP = 200


beta_one = 0.9
beta_two = 0.999
learn_rate = 0.003
adam_eps = 1e-08
factor_scale = 2.0

CHUNKS = ((16, 2), (12, 3), (0, 4), (4, 4), (8, 4), (18, 2), (15, 1))
VMEM_BYTES = 40 * 1024 * 1024
WEIGHT = 5


def apply_adam_rule(weights, moment, second, grads):
    moment_new = beta_one * moment + (1.0 - beta_one) * grads
    second_new = beta_two * second + (1.0 - beta_two) * grads * grads
    first_fix = 1.0 - beta_one**ADAM_STEP
    second_fix = 1.0 - beta_two**ADAM_STEP
    step_size = moment_new / first_fix / (jnp.sqrt(second_new / second_fix) + adam_eps)
    return (weights - learn_rate * step_size, moment_new, second_new)


def scatter_sum_rep(part):
    reps = lax.axis_size("rep")
    me = lax.axis_index("rep")
    share = part.shape[0] // reps
    blocks = part.reshape(reps, share, part.shape[1])
    bit = 1
    while bit < reps:
        pairs = blocks.reshape(blocks.shape[0] // 2, 2, share, part.shape[1])
        mine_bit = (me // bit) % 2
        keep = lax.dynamic_index_in_dim(pairs, mine_bit, 1, keepdims=False)
        send = lax.dynamic_index_in_dim(pairs, 1 - mine_bit, 1, keepdims=False)
        got = lax.ppermute(send.astype(jnp.bfloat16), "rep", [(i, i ^ bit) for i in range(reps)])
        blocks = keep + got.astype(jnp.float32)
        bit *= 2
    return blocks[0]


def split_high_low(values):
    high = values.astype(jnp.bfloat16)
    low = (values - high.astype(jnp.float32)).astype(jnp.bfloat16)
    return high, low


def local_any(
    base,
    decoded_row_activations,
    input_factor,
    output_factor,
    input_first_moment,
    input_second_moment,
    output_first_moment,
    output_second_moment,
    replica_input_gradient,
    replica_output_gradient,
):
    x = decoded_row_activations
    width = base.shape[1]
    features = base.shape[0]
    reps = lax.axis_size("rep")
    part = jnp.concatenate([replica_input_gradient[0].T, replica_output_gradient[0]], axis=1)
    grads = scatter_sum_rep(part)
    grads_in, grads_out = grads[:, :features], grads[:, features:]
    new_in, first_in, second_in = apply_adam_rule(input_factor.T, input_first_moment.T, input_second_moment.T, grads_in)
    new_out, first_out, second_out = apply_adam_rule(output_factor, output_first_moment, output_second_moment, grads_out)
    half_in = new_in.astype(jnp.bfloat16)
    half_out = new_out.astype(jnp.bfloat16)
    inner = lax.dot_general(x, half_in, (((1,), (1,)), ((), ())), preferred_element_type=jnp.float32)
    inner = lax.psum_scatter(inner, "tp", scatter_dimension=0, tiled=True)
    inner = lax.all_gather(inner, "rep", axis=1, tiled=True)
    gathered = lax.all_gather(half_out, ("rep", "tp"), axis=1, tiled=True)
    stacked = gathered.reshape(half_out.shape[0], reps, -1)
    full_out = jnp.transpose(stacked, (1, 0, 2)).reshape(half_out.shape[0] * reps, -1)
    full_out = lax.dynamic_slice_in_dim(full_out, lax.axis_index("rep") * width, width, 1)
    high, low = split_high_low(factor_scale * inner)
    spread = jnp.concatenate([high, low], axis=1)
    doubled = jnp.concatenate([full_out, full_out], axis=0)
    partial = jnp.dot(x, base, preferred_element_type=jnp.float32)
    summed = lax.psum_scatter(partial, "tp", scatter_dimension=0, tiled=True)
    decoded = summed + jnp.dot(spread, doubled, preferred_element_type=jnp.float32)
    return (decoded, new_in.T, new_out, first_in.T, second_in.T, first_out, second_out)


LINE = (((0, 1), (3, 2)), ((1, 2), (2, 1)), ((2, 3), (1, 0)))
(SEND_ROW, SECOND_AT, THIRD_AT, THIRD_FROM, OWN, FIRST_OWN, SECOND_OWN, ORDER, CORE_BIT, CHIP_BIT) = (
    0, 1, 2, 3, 4, 5, 6, 7, 11, 12)
MOST = 2048


def place_numbers(share):
    me, rep = lax.axis_index("tp"), lax.axis_index("rep")
    low = me < 2
    order = [me, me ^ 1, jnp.where(low, 2, 1), jnp.where(low, 3, 0)]
    numbers = [
        jnp.where(me == 0, share, 0),
        jnp.where(me == 1, 1, 0),
        jnp.where(me == 2, 3, 0),
        jnp.where(me == 2, 1, 0),
        me,
        jnp.where(me == 1, 0, 2),
        jnp.where(me == 2, 0, 1),
    ]
    numbers += [rank ^ rep for rank in order] + [rep & 1, rep >> 1]
    return jnp.stack([jnp.asarray(n, jnp.int32) for n in numbers])


def call(body, place, operands, specs, earlier, out_shapes, out_specs, grid=(1,), flops=0, moved=0):
    count = len(operands)

    def kernel(place_ref, *refs):
        body(place_ref, *refs[:count], *refs[count + len(earlier):])

    return pl.pallas_call(
        kernel,
        grid_spec=pltpu.PrefetchScalarGridSpec(
            num_scalar_prefetch=1,
            grid=grid,
            in_specs=list(specs) + [pl.BlockSpec(memory_space=pl.ANY)] * len(earlier),
            out_specs=out_specs,
        ),
        out_shape=out_shapes,
        compiler_params=pltpu.CompilerParams(vmem_limit_bytes=VMEM_BYTES),
        cost_estimate=pl.CostEstimate(flops=WEIGHT * flops, bytes_accessed=WEIGHT * moved, transcendentals=0),
    )(place, *operands, *earlier)


def whole(shape):
    return pl.BlockSpec(shape, lambda *_: (0,) * len(shape))


def block_width(start, width, most):
    block = min(most, width)
    while start % block or width % block:
        block //= 2
    return block


def matmul_chunk(place, x, base, start, width, share, earlier, most):
    rows, depth = x.shape
    block = block_width(start, width, most)
    sent = rows - share

    def body(place_ref, x_ref, base_ref, partial_ref, send_ref):
        partial_ref[...] = jnp.dot(x_ref[...], base_ref[...], preferred_element_type=jnp.float32)
        row = pl.multiple_of(place_ref[SEND_ROW], share)
        send_ref[...] = partial_ref[pl.ds(row, sent), :].astype(jnp.bfloat16)

    return call(
        body,
        place,
        [x, base],
        [whole(x.shape), pl.BlockSpec((depth, block), lambda j, p: (0, start // block + j))],
        earlier,
        [jax.ShapeDtypeStruct((rows, width), jnp.float32), jax.ShapeDtypeStruct((sent, width), jnp.bfloat16)],
        [pl.BlockSpec((rows, block), lambda j, p: (0, j)), pl.BlockSpec((sent, block), lambda j, p: (0, j))],
        grid=(width // block,),
        flops=2 * rows * depth * width,
        moved=2 * depth * width,
    )


def add_second(place, pieces, share, earlier):
    operands, specs = [], []
    for partial, arrived in pieces:
        width = partial.shape[1]
        operands += [partial, arrived, arrived]
        specs += [
            pl.BlockSpec((2 * share, width), lambda j, p: (p[SECOND_AT], 0)),
            pl.BlockSpec((share, width), lambda j, p: (p[SECOND_AT], 0)),
            pl.BlockSpec((share, width), lambda j, p: (p[SECOND_AT] + 1, 0)),
        ]
    widths = [partial.shape[1] for partial, _ in pieces]

    def body(place_ref, *refs):
        out_ref, at = refs[-1], 0
        for i, width in enumerate(widths):
            partial_ref, upper_ref, lower_ref = refs[3 * i:3 * i + 3]
            to = slice(at, at + width)
            out_ref[:share, to] = (partial_ref[:share, :] + upper_ref[...].astype(jnp.float32)).astype(jnp.bfloat16)
            out_ref[share:, to] = (partial_ref[share:, :] + lower_ref[...].astype(jnp.float32)).astype(jnp.bfloat16)
            at += width

    shape = (2 * share, sum(widths))
    return call(
        body, place, operands, specs, earlier, jax.ShapeDtypeStruct(shape, jnp.bfloat16), whole(shape),
        moved=16 * share * shape[1],
    )


def add_third(place, pieces, share, earlier):
    operands, specs = [], []
    for partial, arrived, _ in pieces:
        operands += [partial, arrived]
        specs += [
            pl.BlockSpec((share, partial.shape[1]), lambda j, p: (p[THIRD_AT], 0)),
            pl.BlockSpec((share, arrived.shape[1]), lambda j, p: (p[THIRD_FROM], 0)),
        ]
    widths = [partial.shape[1] for partial, _, _ in pieces]
    inside = [at for _, _, at in pieces]

    def body(place_ref, *refs):
        out_ref, at = refs[-1], 0
        for i, width in enumerate(widths):
            partial_ref, arrived_ref = refs[2 * i:2 * i + 2]
            arrived = arrived_ref[:, inside[i]:inside[i] + width].astype(jnp.float32)
            out_ref[:, at:at + width] = (partial_ref[...] + arrived).astype(jnp.bfloat16)
            at += width

    shape = (share, sum(widths))
    return call(
        body, place, operands, specs, earlier, jax.ShapeDtypeStruct(shape, jnp.bfloat16), whole(shape),
        moved=8 * share * shape[1],
    )


def finish_chunks(place, pieces, spread, factors, share, earlier, full_width=None, done=()):
    operands, specs = [spread], [whole(spread.shape)]
    half = factors[0].shape[0]
    for start, partial, first, second, _, third, _ in pieces:
        width = partial.shape[1]
        operands += [partial, first, second, third, *factors]
        specs += [
            pl.BlockSpec((share, width), lambda j, p: (p[OWN], 0)),
            pl.BlockSpec((share, width), lambda j, p: (p[FIRST_OWN], 0)),
            pl.BlockSpec((share, second.shape[1]), lambda j, p: (p[SECOND_OWN], 0)),
            whole(third.shape),
        ] + [pl.BlockSpec((half, width), lambda j, p, at=start // width: (0, at))] * 3
    for columns, _ in done:
        operands.append(columns)
        specs.append(whole(columns.shape))
    places = [(start, partial.shape[1], two, three) for start, partial, _, _, two, _, three in pieces]
    shape = (share, sum(width for _, width, _, _ in places) if full_width is None else full_width)

    def body(place_ref, spread_ref, *refs):
        out_ref, at = refs[-1], 0
        for i, (start, width, two, three) in enumerate(places):
            own_ref, first_ref, second_ref, third_ref, pair_ref, near_ref, far_ref = refs[7 * i:7 * i + 7]
            other = near_ref[...] + far_ref[...]
            ranks = jnp.concatenate([pair_ref[...], other, pair_ref[...], other], axis=0)
            total = own_ref[...] + first_ref[...].astype(jnp.float32)
            total = total + second_ref[:, two:two + width].astype(jnp.float32)
            total = total + third_ref[:, three:three + width].astype(jnp.float32)
            total = total + jnp.dot(spread_ref[...], ranks, preferred_element_type=jnp.float32)
            to = at if full_width is None else start
            out_ref[:, to:to + width] = total
            at += width
        for ref, (_, parts) in zip(refs[7 * len(places):], done):
            at = 0
            for start, width in parts:
                out_ref[:, start:start + width] = ref[:, at:at + width]
                at += width

    return call(
        body, place, operands, specs, earlier, jax.ShapeDtypeStruct(shape, jnp.float32), whole(shape),
        moved=14 * share * shape[1],
    )


def gradients_out(place, part_in, part_out, earlier):
    features, columns = part_in.shape[3], part_out.shape[3]
    rows = 2 * part_in.shape[2]

    def body(place_ref, in_ref, out_ref, send_ref):
        send_ref[:, :features] = in_ref[...].reshape(rows, features).astype(jnp.bfloat16)
        send_ref[:, features:] = out_ref[...].reshape(rows, columns).astype(jnp.bfloat16)

    shape = (rows, features + columns)
    return call(
        body,
        place,
        [part_in, part_out],
        [
            pl.BlockSpec((2, 1, rows // 2, n), lambda j, p: (0, 1 - p[CORE_BIT], 0, 0))
            for n in (features, columns)
        ],
        earlier,
        jax.ShapeDtypeStruct(shape, jnp.bfloat16),
        whole(shape),
        moved=6 * shape[0] * shape[1],
    )


def gradients_on(place, part_in, part_out, arrived, earlier):
    features, columns = part_in.shape[3], part_out.shape[3]
    ranks = part_in.shape[2]

    def body(place_ref, in_ref, out_ref, arrived_ref, send_ref, keep_ref):
        upper = place_ref[CHIP_BIT] == 0
        for ref, at, n in ((in_ref, 0, features), (out_ref, features, columns)):
            total = ref[...].reshape(2 * ranks, n) + arrived_ref[:, at:at + n].astype(jnp.float32)
            keep_ref[:, at:at + n] = jnp.where(upper, total[:ranks], total[ranks:])
            send_ref[:, at:at + n] = jnp.where(upper, total[ranks:], total[:ranks]).astype(jnp.bfloat16)

    shape = (ranks, features + columns)
    return call(
        body,
        place,
        [part_in, part_out, arrived],
        [pl.BlockSpec((2, 1, ranks, n), lambda j, p: (0, p[CORE_BIT], 0, 0)) for n in (features, columns)]
        + [whole(arrived.shape)],
        earlier,
        [jax.ShapeDtypeStruct(shape, jnp.bfloat16), jax.ShapeDtypeStruct(shape, jnp.float32)],
        [whole(shape)] * 2,
        moved=20 * shape[0] * shape[1],
    )


def update_factors(place, keep, arrived, in_state, out_state, earlier):
    features, columns = in_state[0].shape[1], out_state[0].shape[1]
    ranks = keep.shape[0]

    def body(place_ref, keep_ref, arrived_ref, *refs):
        for side, at, n in ((0, 0, features), (1, features, columns)):
            weights, first, second = refs[3 * side:3 * side + 3]
            outs = refs[6 + 4 * side:10 + 4 * side]
            grads = keep_ref[:, at:at + n] + arrived_ref[:, at:at + n].astype(jnp.float32)
            values = apply_adam_rule(weights[...], first[...], second[...], grads)
            for out, value in zip(outs, values):
                out[...] = value
            outs[3][...] = values[0].astype(jnp.bfloat16)

    operands = [keep, arrived, *in_state, *out_state]
    shapes = []
    for n in (features, columns):
        shapes += [jax.ShapeDtypeStruct((ranks, n), jnp.float32)] * 3 + [jax.ShapeDtypeStruct((ranks, n), jnp.bfloat16)]
    return call(
        body,
        place,
        operands,
        [whole(o.shape) for o in operands],
        earlier,
        shapes,
        [whole(s.shape) for s in shapes],
        moved=32 * ranks * (features + columns),
    )


def inner_products(place, x, near, far, turned, earlier):
    rows, ranks = x.shape[0], turned.shape[0]
    width = turned.shape[1]
    inner_width = 4 * rows

    def body(place_ref, x_ref, near_ref, far_ref, turned_ref, inner_ref, send_ref):
        for i, ref in enumerate((near_ref, far_ref)):
            products = lax.dot_general(
                ref[...], x_ref[...], (((1,), (1,)), ((), ())), preferred_element_type=jnp.float32
            )
            for j in range(2):
                at = (2 * i + j) * rows
                inner_ref[:, at:at + rows] = products[j * ranks:(j + 1) * ranks]
        high, low = split_high_low(inner_ref[...])
        send_ref[:, :width] = turned_ref[...]
        send_ref[:, width:width + inner_width] = high
        send_ref[:, width + inner_width:] = low

    shapes = [(ranks, inner_width), (ranks, width + 2 * inner_width)]
    return call(
        body,
        place,
        [x, near, far, turned],
        [whole(x.shape), whole(near.shape), whole(far.shape), whole(turned.shape)],
        earlier,
        [jax.ShapeDtypeStruct(shapes[0], jnp.float32), jax.ShapeDtypeStruct(shapes[1], jnp.bfloat16)],
        [whole(shape) for shape in shapes],
        flops=8 * rows * ranks * x.shape[1],
        moved=2 * rows * x.shape[1],
    )


def join_pair(place, turned, swapped, inner, earlier):
    ranks, width = turned.shape
    inner_width = inner.shape[1]

    def body(place_ref, turned_ref, swapped_ref, inner_ref, pair_ref, sum_ref):
        both = [turned_ref[...].astype(jnp.float32), swapped_ref[:, :width].astype(jnp.float32)]
        pair_ref[:, :width] = jnp.concatenate(both, axis=0).astype(jnp.bfloat16)
        total = inner_ref[...] + swapped_ref[:, width:width + inner_width].astype(jnp.float32)
        total = total + swapped_ref[:, width + inner_width:].astype(jnp.float32)
        sum_ref[...] = total
        halves = [half.astype(jnp.float32) for half in split_high_low(total)]
        pair_ref[:, width:] = jnp.concatenate(halves, axis=0).astype(jnp.bfloat16)

    shapes = [(2 * ranks, width + inner_width), (ranks, inner_width)]
    return call(
        body,
        place,
        [turned, swapped, inner],
        [whole(turned.shape), whole(swapped.shape), whole(inner.shape)],
        earlier,
        [jax.ShapeDtypeStruct(shapes[0], jnp.bfloat16), jax.ShapeDtypeStruct(shapes[1], jnp.float32)],
        [whole(shape) for shape in shapes],
        moved=8 * ranks * width,
    )


def spread_inner(place, inner, near, far, width, share, earlier):
    portion = inner.shape[0]
    rows = inner.shape[1] // 4
    ranks = 4 * portion

    def body(place_ref, inner_ref, near_ref, far_ref, out_ref):
        other = near_ref[:, width:].astype(jnp.float32) + far_ref[:, width:].astype(jnp.float32)
        total = factor_scale * (inner_ref[...] + (other[:portion] + other[portion:]))
        total = jnp.concatenate([total[:, i * rows:(i + 1) * rows] for i in range(4)], axis=0)
        shape = (share, rows)
        mine = lax.broadcasted_iota(jnp.int32, shape, 0) + place_ref[OWN] * share
        mine = jnp.where(lax.broadcasted_iota(jnp.int32, shape, 1) == mine, 1.0, 0.0).astype(jnp.bfloat16)
        block = lax.broadcasted_iota(jnp.int32, (ranks, ranks), 1) // portion
        source = jnp.full((ranks, ranks), 0, jnp.int32)
        for i in range(4):
            source = jnp.where(block == i, place_ref[ORDER + i], source)
        column = lax.broadcasted_iota(jnp.int32, (ranks, ranks), 1) % portion
        chosen = lax.broadcasted_iota(jnp.int32, (ranks, ranks), 0) == source * portion + column
        chosen = jnp.where(chosen, 1.0, 0.0).astype(jnp.bfloat16)
        halves = []
        for half in split_high_low(total):
            turned = lax.dot_general(mine, half, (((1,), (1,)), ((), ())), preferred_element_type=jnp.float32)
            halves.append(jnp.dot(turned.astype(jnp.bfloat16), chosen, preferred_element_type=jnp.float32))
        out_ref[...] = jnp.concatenate(halves, axis=1).astype(jnp.bfloat16)

    return call(
        body,
        place,
        [inner, near, far],
        [whole(inner.shape), whole(near.shape), whole(far.shape)],
        earlier,
        jax.ShapeDtypeStruct((share, 2 * ranks), jnp.bfloat16),
        whole((share, 2 * ranks)),
    )


def local_line(
    base,
    decoded_row_activations,
    input_factor,
    output_factor,
    input_first_moment,
    input_second_moment,
    output_first_moment,
    output_second_moment,
    replica_input_gradient,
    replica_output_gradient,
):
    x = decoded_row_activations
    width = base.shape[1]
    share = x.shape[0] // 4
    ranks = input_factor.shape[1]
    place = place_numbers(share)
    part_in = replica_input_gradient[0].T.reshape(2, 2, ranks, -1)
    part_out = replica_output_gradient[0].reshape(2, 2, ranks, -1)

    unit = width // 20
    starts = [unit * at for at, _ in CHUNKS]
    widths = [unit * wide for _, wide in CHUNKS]
    partials, firsts, seconds, thirds = {}, {}, {}, {}

    def line(step, values):
        return lax.ppermute(values, "tp", LINE[step])

    def chip(bit, values):
        return lax.ppermute(values, "rep", [(i, i ^ bit) for i in range(4)])

    def matmul(c, *earlier):
        partials[c], send = matmul_chunk(place, x, base, starts[c], widths[c], share, earlier, 512)
        firsts[c] = line(0, send)
        return send

    def second(chunks, *earlier):
        send = add_second(place, [(partials[c], firsts[c]) for c in chunks], share, earlier)
        got, at = line(1, send), 0
        for c in chunks:
            seconds[c] = (got, at)
            at += widths[c]
        return send

    def third(chunks, *earlier):
        send = add_third(place, [(partials[c], *seconds[c]) for c in chunks], share, earlier)
        got, at = line(2, send), 0
        for c in chunks:
            thirds[c] = (got, at)
            at += widths[c]
        return send

    def finish(chunks, *earlier, full_width=None, done=()):
        pieces = [(starts[c], partials[c], firsts[c], *seconds[c], *thirds[c]) for c in chunks]
        columns = finish_chunks(place, pieces, spread, factors, share, earlier, full_width, done)
        finished.append((columns, [(starts[c], widths[c]) for c in chunks]))
        return columns

    finished = []
    last = matmul(0)
    last = gradients_out(place, part_in, part_out, [last])
    from_core = chip(1, last)
    last = matmul(1, last)
    across, keep = gradients_on(place, part_in, part_out, from_core, [last])
    from_chip = chip(2, across)
    last = matmul(2, keep)
    in_state = (input_factor.T, input_first_moment.T, input_second_moment.T)
    out_state = (output_factor, output_first_moment, output_second_moment)
    states = update_factors(place, keep, from_chip, in_state, out_state, [last])
    new_in, first_in, second_in, half_in, new_out, first_out, second_out, half_out = states
    turned = lax.ppermute(half_out, ("rep", "tp"), [(4 * a + b, 4 * b + a) for a in range(4) for b in range(4)])
    near_in = jnp.concatenate([half_in, chip(1, half_in)], axis=0)
    far_in = chip(2, near_in)
    last = second((0, 1), half_out)
    last = matmul(3, last)
    inner, last = inner_products(place, x, near_in, far_in, turned, [last])
    swapped = lax.ppermute(last, "tp", [(i, i ^ 1) for i in range(4)])
    last = second((2,), last)
    last = matmul(4, last)
    last = second((3,), last)
    last = third((0, 1, 2), last)
    pair, inner = join_pair(place, turned, swapped, inner, [last])
    near_out = line(1, pair)
    last = matmul(5, pair)
    last = matmul(6, last)
    last = second((4,), last, thirds[0][0])
    far_out = line(2, near_out)
    factors = (pair, near_out, far_out)
    last = second((5,), last)
    last = third((3,), last)
    last = second((6,), last)
    last = third((4,), last)
    last = third((5, 6), last)
    last = spread = spread_inner(place, inner, near_out, far_out, width, share, [last])
    last = finish((0, 1, 2), last)
    last = finish((3,), last)
    last = finish((4,), last)
    decoded = finish((5, 6), last, full_width=width, done=list(finished))
    return (decoded, new_in.T, new_out, first_in.T, second_in.T, first_out, second_out)


def solution(mesh):
    line = mesh.shape["rep"] == 4 and mesh.shape["tp"] == 4
    return jax.shard_map(
        local_line if line else local_any,
        mesh=mesh,
        in_specs=(
            P("tp", "rep"),
            P("groups", "tp"),
            P(("groups", "tp"), "rep"),
            P("rep", ("groups", "tp")),
            P(("groups", "tp"), "rep"),
            P(("groups", "tp"), "rep"),
            P("rep", ("groups", "tp")),
            P("rep", ("groups", "tp")),
            P("rep", ("groups", "tp"), None),
            P("rep", None, ("groups", "tp")),
        ),
        out_specs=(
            P(("groups", "tp"), "rep"),
            P(("groups", "tp"), "rep"),
            P("rep", ("groups", "tp")),
            P(("groups", "tp"), "rep"),
            P(("groups", "tp"), "rep"),
            P("rep", ("groups", "tp")),
            P("rep", ("groups", "tp")),
        ),
        check_vma=False,
    )
```

```python
import jax
import jax.numpy as jnp
from jax import lax
from jax.experimental import pallas as pl
from jax.experimental.pallas import tpu as pltpu
from jax.sharding import PartitionSpec as P

ADAM_STEP = 200


beta_one = 0.9
beta_two = 0.999
learn_rate = 0.003
adam_eps = 1e-08
factor_scale = 2.0

CHUNKS = ((16, 2), (12, 3), (0, 4), (4, 4), (8, 4), (18, 2), (15, 1))
VMEM_BYTES = 40 * 1024 * 1024
WEIGHT = 5


def apply_adam_rule(weights, moment, second, grads):
    moment_new = beta_one * moment + (1.0 - beta_one) * grads
    second_new = beta_two * second + (1.0 - beta_two) * grads * grads
    first_fix = 1.0 - beta_one**ADAM_STEP
    second_fix = 1.0 - beta_two**ADAM_STEP
    step_size = moment_new / first_fix / (jnp.sqrt(second_new / second_fix) + adam_eps)
    return (weights - learn_rate * step_size, moment_new, second_new)


def scatter_sum_rep(part):
    reps = lax.axis_size("rep")
    me = lax.axis_index("rep")
    share = part.shape[0] // reps
    blocks = part.reshape(reps, share, part.shape[1])
    bit = 1
    while bit < reps:
        pairs = blocks.reshape(blocks.shape[0] // 2, 2, share, part.shape[1])
        mine_bit = (me // bit) % 2
        keep = lax.dynamic_index_in_dim(pairs, mine_bit, 1, keepdims=False)
        send = lax.dynamic_index_in_dim(pairs, 1 - mine_bit, 1, keepdims=False)
        got = lax.ppermute(send.astype(jnp.bfloat16), "rep", [(i, i ^ bit) for i in range(reps)])
        blocks = keep + got.astype(jnp.float32)
        bit *= 2
    return blocks[0]


def split_high_low(values):
    high = values.astype(jnp.bfloat16)
    low = (values - high.astype(jnp.float32)).astype(jnp.bfloat16)
    return high, low


def local_any(
    base,
    decoded_row_activations,
    input_factor,
    output_factor,
    input_first_moment,
    input_second_moment,
    output_first_moment,
    output_second_moment,
    replica_input_gradient,
    replica_output_gradient,
):
    x = decoded_row_activations
    width = base.shape[1]
    features = base.shape[0]
    reps = lax.axis_size("rep")
    part = jnp.concatenate([replica_input_gradient[0].T, replica_output_gradient[0]], axis=1)
    grads = scatter_sum_rep(part)
    grads_in, grads_out = grads[:, :features], grads[:, features:]
    new_in, first_in, second_in = apply_adam_rule(input_factor.T, input_first_moment.T, input_second_moment.T, grads_in)
    new_out, first_out, second_out = apply_adam_rule(output_factor, output_first_moment, output_second_moment, grads_out)
    half_in = new_in.astype(jnp.bfloat16)
    half_out = new_out.astype(jnp.bfloat16)
    inner = lax.dot_general(x, half_in, (((1,), (1,)), ((), ())), preferred_element_type=jnp.float32)
    inner = lax.psum_scatter(inner, "tp", scatter_dimension=0, tiled=True)
    inner = lax.all_gather(inner, "rep", axis=1, tiled=True)
    gathered = lax.all_gather(half_out, ("rep", "tp"), axis=1, tiled=True)
    stacked = gathered.reshape(half_out.shape[0], reps, -1)
    full_out = jnp.transpose(stacked, (1, 0, 2)).reshape(half_out.shape[0] * reps, -1)
    full_out = lax.dynamic_slice_in_dim(full_out, lax.axis_index("rep") * width, width, 1)
    high, low = split_high_low(factor_scale * inner)
    spread = jnp.concatenate([high, low], axis=1)
    doubled = jnp.concatenate([full_out, full_out], axis=0)
    partial = jnp.dot(x, base, preferred_element_type=jnp.float32)
    summed = lax.psum_scatter(partial, "tp", scatter_dimension=0, tiled=True)
    decoded = summed + jnp.dot(spread, doubled, preferred_element_type=jnp.float32)
    return (decoded, new_in.T, new_out, first_in.T, second_in.T, first_out, second_out)


LINE = (((0, 1), (3, 2)), ((1, 2), (2, 1)), ((2, 3), (1, 0)))
(SEND_ROW, SECOND_AT, THIRD_AT, THIRD_FROM, OWN, FIRST_OWN, SECOND_OWN, ORDER, CORE_BIT, CHIP_BIT) = (
    0, 1, 2, 3, 4, 5, 6, 7, 11, 12)
MOST = 2048


def place_numbers(share):
    me, rep = lax.axis_index("tp"), lax.axis_index("rep")
    low = me < 2
    order = [me, me ^ 1, jnp.where(low, 2, 1), jnp.where(low, 3, 0)]
    numbers = [
        jnp.where(me == 0, share, 0),
        jnp.where(me == 1, 1, 0),
        jnp.where(me == 2, 3, 0),
        jnp.where(me == 2, 1, 0),
        me,
        jnp.where(me == 1, 0, 2),
        jnp.where(me == 2, 0, 1),
    ]
    numbers += [rank ^ rep for rank in order] + [rep & 1, rep >> 1]
    return jnp.stack([jnp.asarray(n, jnp.int32) for n in numbers])


def call(body, place, operands, specs, earlier, out_shapes, out_specs, grid=(1,), flops=0, moved=0):
    count = len(operands)

    def kernel(place_ref, *refs):
        body(place_ref, *refs[:count], *refs[count + len(earlier):])

    return pl.pallas_call(
        kernel,
        grid_spec=pltpu.PrefetchScalarGridSpec(
            num_scalar_prefetch=1,
            grid=grid,
            in_specs=list(specs) + [pl.BlockSpec(memory_space=pl.ANY)] * len(earlier),
            out_specs=out_specs,
        ),
        out_shape=out_shapes,
        compiler_params=pltpu.CompilerParams(vmem_limit_bytes=VMEM_BYTES),
        cost_estimate=pl.CostEstimate(flops=WEIGHT * flops, bytes_accessed=WEIGHT * moved, transcendentals=0),
    )(place, *operands, *earlier)


def whole(shape):
    return pl.BlockSpec(shape, lambda *_: (0,) * len(shape))


def block_width(start, width, most):
    block = min(most, width)
    while start % block or width % block:
        block //= 2
    return block


def matmul_chunk(place, x, base, start, width, share, earlier, most):
    rows, depth = x.shape
    block = block_width(start, width, most)
    sent = rows - share

    def body(place_ref, x_ref, base_ref, partial_ref, send_ref):
        partial_ref[...] = jnp.dot(x_ref[...], base_ref[...], preferred_element_type=jnp.float32)
        row = pl.multiple_of(place_ref[SEND_ROW], share)
        send_ref[...] = partial_ref[pl.ds(row, sent), :].astype(jnp.bfloat16)

    return call(
        body,
        place,
        [x, base],
        [whole(x.shape), pl.BlockSpec((depth, block), lambda j, p: (0, start // block + j))],
        earlier,
        [jax.ShapeDtypeStruct((rows, width), jnp.float32), jax.ShapeDtypeStruct((sent, width), jnp.bfloat16)],
        [pl.BlockSpec((rows, block), lambda j, p: (0, j)), pl.BlockSpec((sent, block), lambda j, p: (0, j))],
        grid=(width // block,),
        flops=2 * rows * depth * width,
        moved=2 * depth * width,
    )


def add_second(place, pieces, share, earlier):
    operands, specs = [], []
    for partial, arrived in pieces:
        width = partial.shape[1]
        operands += [partial, arrived, arrived]
        specs += [
            pl.BlockSpec((2 * share, width), lambda j, p: (p[SECOND_AT], 0)),
            pl.BlockSpec((share, width), lambda j, p: (p[SECOND_AT], 0)),
            pl.BlockSpec((share, width), lambda j, p: (p[SECOND_AT] + 1, 0)),
        ]
    widths = [partial.shape[1] for partial, _ in pieces]

    def body(place_ref, *refs):
        out_ref, at = refs[-1], 0
        for i, width in enumerate(widths):
            partial_ref, upper_ref, lower_ref = refs[3 * i:3 * i + 3]
            to = slice(at, at + width)
            out_ref[:share, to] = (partial_ref[:share, :] + upper_ref[...].astype(jnp.float32)).astype(jnp.bfloat16)
            out_ref[share:, to] = (partial_ref[share:, :] + lower_ref[...].astype(jnp.float32)).astype(jnp.bfloat16)
            at += width

    shape = (2 * share, sum(widths))
    return call(
        body, place, operands, specs, earlier, jax.ShapeDtypeStruct(shape, jnp.bfloat16), whole(shape),
        moved=16 * share * shape[1],
    )


def add_third(place, pieces, share, earlier):
    operands, specs = [], []
    for partial, arrived, _ in pieces:
        operands += [partial, arrived]
        specs += [
            pl.BlockSpec((share, partial.shape[1]), lambda j, p: (p[THIRD_AT], 0)),
            pl.BlockSpec((share, arrived.shape[1]), lambda j, p: (p[THIRD_FROM], 0)),
        ]
    widths = [partial.shape[1] for partial, _, _ in pieces]
    inside = [at for _, _, at in pieces]

    def body(place_ref, *refs):
        out_ref, at = refs[-1], 0
        for i, width in enumerate(widths):
            partial_ref, arrived_ref = refs[2 * i:2 * i + 2]
            arrived = arrived_ref[:, inside[i]:inside[i] + width].astype(jnp.float32)
            out_ref[:, at:at + width] = (partial_ref[...] + arrived).astype(jnp.bfloat16)
            at += width

    shape = (share, sum(widths))
    return call(
        body, place, operands, specs, earlier, jax.ShapeDtypeStruct(shape, jnp.bfloat16), whole(shape),
        moved=8 * share * shape[1],
    )


def finish_chunks(place, pieces, spread, factors, share, earlier, full_width=None, done=()):
    operands, specs = [spread], [whole(spread.shape)]
    half = factors[0].shape[0]
    for start, partial, first, second, _, third, _ in pieces:
        width = partial.shape[1]
        operands += [partial, first, second, third, *factors]
        specs += [
            pl.BlockSpec((share, width), lambda j, p: (p[OWN], 0)),
            pl.BlockSpec((share, width), lambda j, p: (p[FIRST_OWN], 0)),
            pl.BlockSpec((share, second.shape[1]), lambda j, p: (p[SECOND_OWN], 0)),
            whole(third.shape),
        ] + [pl.BlockSpec((half, width), lambda j, p, at=start // width: (0, at))] * 3
    for columns, _ in done:
        operands.append(columns)
        specs.append(whole(columns.shape))
    places = [(start, partial.shape[1], two, three) for start, partial, _, _, two, _, three in pieces]
    shape = (share, sum(width for _, width, _, _ in places) if full_width is None else full_width)

    def body(place_ref, spread_ref, *refs):
        out_ref, at = refs[-1], 0
        for i, (start, width, two, three) in enumerate(places):
            own_ref, first_ref, second_ref, third_ref, pair_ref, near_ref, far_ref = refs[7 * i:7 * i + 7]
            other = near_ref[...] + far_ref[...]
            ranks = jnp.concatenate([pair_ref[...], other, pair_ref[...], other], axis=0)
            total = own_ref[...] + first_ref[...].astype(jnp.float32)
            total = total + second_ref[:, two:two + width].astype(jnp.float32)
            total = total + third_ref[:, three:three + width].astype(jnp.float32)
            total = total + jnp.dot(spread_ref[...], ranks, preferred_element_type=jnp.float32)
            to = at if full_width is None else start
            out_ref[:, to:to + width] = total
            at += width
        for ref, (_, parts) in zip(refs[7 * len(places):], done):
            at = 0
            for start, width in parts:
                out_ref[:, start:start + width] = ref[:, at:at + width]
                at += width

    return call(
        body, place, operands, specs, earlier, jax.ShapeDtypeStruct(shape, jnp.float32), whole(shape),
        moved=14 * share * shape[1],
    )


def gradients_out(place, part_in, part_out, earlier):
    features, columns = part_in.shape[3], part_out.shape[3]
    rows = 2 * part_in.shape[2]

    def body(place_ref, in_ref, out_ref, send_ref):
        send_ref[:, :features] = in_ref[...].reshape(rows, features).astype(jnp.bfloat16)
        send_ref[:, features:] = out_ref[...].reshape(rows, columns).astype(jnp.bfloat16)

    shape = (rows, features + columns)
    return call(
        body,
        place,
        [part_in, part_out],
        [
            pl.BlockSpec((2, 1, rows // 2, n), lambda j, p: (0, 1 - p[CORE_BIT], 0, 0))
            for n in (features, columns)
        ],
        earlier,
        jax.ShapeDtypeStruct(shape, jnp.bfloat16),
        whole(shape),
        moved=6 * shape[0] * shape[1],
    )


def gradients_on(place, part_in, part_out, arrived, earlier):
    features, columns = part_in.shape[3], part_out.shape[3]
    ranks = part_in.shape[2]

    def body(place_ref, in_ref, out_ref, arrived_ref, send_ref, keep_ref):
        upper = place_ref[CHIP_BIT] == 0
        for ref, at, n in ((in_ref, 0, features), (out_ref, features, columns)):
            total = ref[...].reshape(2 * ranks, n) + arrived_ref[:, at:at + n].astype(jnp.float32)
            keep_ref[:, at:at + n] = jnp.where(upper, total[:ranks], total[ranks:])
            send_ref[:, at:at + n] = jnp.where(upper, total[ranks:], total[:ranks]).astype(jnp.bfloat16)

    shape = (ranks, features + columns)
    return call(
        body,
        place,
        [part_in, part_out, arrived],
        [pl.BlockSpec((2, 1, ranks, n), lambda j, p: (0, p[CORE_BIT], 0, 0)) for n in (features, columns)]
        + [whole(arrived.shape)],
        earlier,
        [jax.ShapeDtypeStruct(shape, jnp.bfloat16), jax.ShapeDtypeStruct(shape, jnp.float32)],
        [whole(shape)] * 2,
        moved=20 * shape[0] * shape[1],
    )


def update_factors(place, keep, arrived, in_state, out_state, earlier):
    features, columns = in_state[0].shape[1], out_state[0].shape[1]
    ranks = keep.shape[0]

    def body(place_ref, keep_ref, arrived_ref, *refs):
        for side, at, n in ((0, 0, features), (1, features, columns)):
            weights, first, second = refs[3 * side:3 * side + 3]
            outs = refs[6 + 4 * side:10 + 4 * side]
            grads = keep_ref[:, at:at + n] + arrived_ref[:, at:at + n].astype(jnp.float32)
            values = apply_adam_rule(weights[...], first[...], second[...], grads)
            for out, value in zip(outs, values):
                out[...] = value
            outs[3][...] = values[0].astype(jnp.bfloat16)

    operands = [keep, arrived, *in_state, *out_state]
    shapes = []
    for n in (features, columns):
        shapes += [jax.ShapeDtypeStruct((ranks, n), jnp.float32)] * 3 + [jax.ShapeDtypeStruct((ranks, n), jnp.bfloat16)]
    return call(
        body,
        place,
        operands,
        [whole(o.shape) for o in operands],
        earlier,
        shapes,
        [whole(s.shape) for s in shapes],
        moved=32 * ranks * (features + columns),
    )


def inner_products(place, x, near, far, turned, earlier):
    rows, ranks = x.shape[0], turned.shape[0]
    width = turned.shape[1]
    inner_width = 4 * rows

    def body(place_ref, x_ref, near_ref, far_ref, turned_ref, inner_ref, send_ref):
        for i, ref in enumerate((near_ref, far_ref)):
            products = lax.dot_general(
                ref[...], x_ref[...], (((1,), (1,)), ((), ())), preferred_element_type=jnp.float32
            )
            for j in range(2):
                at = (2 * i + j) * rows
                inner_ref[:, at:at + rows] = products[j * ranks:(j + 1) * ranks]
        high, low = split_high_low(inner_ref[...])
        send_ref[:, :width] = turned_ref[...]
        send_ref[:, width:width + inner_width] = high
        send_ref[:, width + inner_width:] = low

    shapes = [(ranks, inner_width), (ranks, width + 2 * inner_width)]
    return call(
        body,
        place,
        [x, near, far, turned],
        [whole(x.shape), whole(near.shape), whole(far.shape), whole(turned.shape)],
        earlier,
        [jax.ShapeDtypeStruct(shapes[0], jnp.float32), jax.ShapeDtypeStruct(shapes[1], jnp.bfloat16)],
        [whole(shape) for shape in shapes],
        flops=8 * rows * ranks * x.shape[1],
        moved=2 * rows * x.shape[1],
    )


def join_pair(place, turned, swapped, inner, earlier):
    ranks, width = turned.shape
    inner_width = inner.shape[1]

    def body(place_ref, turned_ref, swapped_ref, inner_ref, pair_ref, sum_ref):
        both = [turned_ref[...].astype(jnp.float32), swapped_ref[:, :width].astype(jnp.float32)]
        pair_ref[:, :width] = jnp.concatenate(both, axis=0).astype(jnp.bfloat16)
        total = inner_ref[...] + swapped_ref[:, width:width + inner_width].astype(jnp.float32)
        total = total + swapped_ref[:, width + inner_width:].astype(jnp.float32)
        sum_ref[...] = total
        halves = [half.astype(jnp.float32) for half in split_high_low(total)]
        pair_ref[:, width:] = jnp.concatenate(halves, axis=0).astype(jnp.bfloat16)

    shapes = [(2 * ranks, width + inner_width), (ranks, inner_width)]
    return call(
        body,
        place,
        [turned, swapped, inner],
        [whole(turned.shape), whole(swapped.shape), whole(inner.shape)],
        earlier,
        [jax.ShapeDtypeStruct(shapes[0], jnp.bfloat16), jax.ShapeDtypeStruct(shapes[1], jnp.float32)],
        [whole(shape) for shape in shapes],
        moved=8 * ranks * width,
    )


def spread_inner(place, inner, near, far, width, share, earlier):
    portion = inner.shape[0]
    rows = inner.shape[1] // 4
    ranks = 4 * portion

    def body(place_ref, inner_ref, near_ref, far_ref, out_ref):
        other = near_ref[:, width:].astype(jnp.float32) + far_ref[:, width:].astype(jnp.float32)
        total = factor_scale * (inner_ref[...] + (other[:portion] + other[portion:]))
        total = jnp.concatenate([total[:, i * rows:(i + 1) * rows] for i in range(4)], axis=0)
        shape = (share, rows)
        mine = lax.broadcasted_iota(jnp.int32, shape, 0) + place_ref[OWN] * share
        mine = jnp.where(lax.broadcasted_iota(jnp.int32, shape, 1) == mine, 1.0, 0.0).astype(jnp.bfloat16)
        block = lax.broadcasted_iota(jnp.int32, (ranks, ranks), 1) // portion
        source = jnp.full((ranks, ranks), 0, jnp.int32)
        for i in range(4):
            source = jnp.where(block == i, place_ref[ORDER + i], source)
        column = lax.broadcasted_iota(jnp.int32, (ranks, ranks), 1) % portion
        chosen = lax.broadcasted_iota(jnp.int32, (ranks, ranks), 0) == source * portion + column
        chosen = jnp.where(chosen, 1.0, 0.0).astype(jnp.bfloat16)
        halves = []
        for half in split_high_low(total):
            turned = lax.dot_general(mine, half, (((1,), (1,)), ((), ())), preferred_element_type=jnp.float32)
            halves.append(jnp.dot(turned.astype(jnp.bfloat16), chosen, preferred_element_type=jnp.float32))
        out_ref[...] = jnp.concatenate(halves, axis=1).astype(jnp.bfloat16)

    return call(
        body,
        place,
        [inner, near, far],
        [whole(inner.shape), whole(near.shape), whole(far.shape)],
        earlier,
        jax.ShapeDtypeStruct((share, 2 * ranks), jnp.bfloat16),
        whole((share, 2 * ranks)),
    )


def local_line(
    base,
    decoded_row_activations,
    input_factor,
    output_factor,
    input_first_moment,
    input_second_moment,
    output_first_moment,
    output_second_moment,
    replica_input_gradient,
    replica_output_gradient,
):
    x = decoded_row_activations
    width = base.shape[1]
    share = x.shape[0] // 4
    ranks = input_factor.shape[1]
    place = place_numbers(share)
    part_in = replica_input_gradient[0].T.reshape(2, 2, ranks, -1)
    part_out = replica_output_gradient[0].reshape(2, 2, ranks, -1)

    unit = width // 20
    starts = [unit * at for at, _ in CHUNKS]
    widths = [unit * wide for _, wide in CHUNKS]
    partials, firsts, seconds, thirds = {}, {}, {}, {}

    def line(step, values):
        return lax.ppermute(values, "tp", LINE[step])

    def chip(bit, values):
        return lax.ppermute(values, "rep", [(i, i ^ bit) for i in range(4)])

    def matmul(c, *earlier):
        partials[c], send = matmul_chunk(place, x, base, starts[c], widths[c], share, earlier, 512)
        firsts[c] = line(0, send)
        return send

    def second(chunks, *earlier):
        send = add_second(place, [(partials[c], firsts[c]) for c in chunks], share, earlier)
        got, at = line(1, send), 0
        for c in chunks:
            seconds[c] = (got, at)
            at += widths[c]
        return send

    def third(chunks, *earlier):
        send = add_third(place, [(partials[c], *seconds[c]) for c in chunks], share, earlier)
        got, at = line(2, send), 0
        for c in chunks:
            thirds[c] = (got, at)
            at += widths[c]
        return send

    def finish(chunks, *earlier, full_width=None, done=()):
        pieces = [(starts[c], partials[c], firsts[c], *seconds[c], *thirds[c]) for c in chunks]
        columns = finish_chunks(place, pieces, spread, factors, share, earlier, full_width, done)
        finished.append((columns, [(starts[c], widths[c]) for c in chunks]))
        return columns

    finished = []
    last = matmul(0)
    last = gradients_out(place, part_in, part_out, [last])
    from_core = chip(1, last)
    last = matmul(1, last)
    across, keep = gradients_on(place, part_in, part_out, from_core, [last])
    from_chip = chip(2, across)
    last = matmul(2, keep)
    in_state = (input_factor.T, input_first_moment.T, input_second_moment.T)
    out_state = (output_factor, output_first_moment, output_second_moment)
    states = update_factors(place, keep, from_chip, in_state, out_state, [last])
    new_in, first_in, second_in, half_in, new_out, first_out, second_out, half_out = states
    turned = lax.ppermute(half_out, ("rep", "tp"), [(4 * a + b, 4 * b + a) for a in range(4) for b in range(4)])
    near_in = jnp.concatenate([half_in, chip(1, half_in)], axis=0)
    far_in = chip(2, near_in)
    last = second((0, 1), half_out)
    last = matmul(3, last)
    inner, last = inner_products(place, x, near_in, far_in, turned, [last])
    swapped = lax.ppermute(last, "tp", [(i, i ^ 1) for i in range(4)])
    last = second((2,), last)
    last = matmul(4, last)
    last = second((3,), last)
    last = third((0, 1, 2), last)
    pair, inner = join_pair(place, turned, swapped, inner, [last])
    near_out = line(1, pair)
    last = matmul(5, pair)
    last = matmul(6, last)
    last = second((4,), last, thirds[0][0])
    far_out = line(2, near_out)
    factors = (pair, near_out, far_out)
    last = second((5,), last)
    last = third((3,), last)
    last = second((6,), last)
    last = spread = spread_inner(place, inner, near_out, far_out, width, share, [last])
    last = finish((0, 1, 2), last)
    last = third((4,), last)
    last = third((5, 6), last)
    last = finish((3,), last)
    last = finish((4,), last)
    decoded = finish((5, 6), last, full_width=width, done=list(finished))
    return (decoded, new_in.T, new_out, first_in.T, second_in.T, first_out, second_out)


def solution(mesh):
    line = mesh.shape["rep"] == 4 and mesh.shape["tp"] == 4
    return jax.shard_map(
        local_line if line else local_any,
        mesh=mesh,
        in_specs=(
            P("tp", "rep"),
            P("groups", "tp"),
            P(("groups", "tp"), "rep"),
            P("rep", ("groups", "tp")),
            P(("groups", "tp"), "rep"),
            P(("groups", "tp"), "rep"),
            P("rep", ("groups", "tp")),
            P("rep", ("groups", "tp")),
            P("rep", ("groups", "tp"), None),
            P("rep", None, ("groups", "tp")),
        ),
        out_specs=(
            P(("groups", "tp"), "rep"),
            P(("groups", "tp"), "rep"),
            P("rep", ("groups", "tp")),
            P(("groups", "tp"), "rep"),
            P(("groups", "tp"), "rep"),
            P("rep", ("groups", "tp")),
            P("rep", ("groups", "tp")),
        ),
        check_vma=False,
    )
```
